128 devices in a mesh: depth: 4 (over y), xline: 32 (over x, z, core).
Axes of the slice: x: 4, y: 4, z: 4, core: 2. Of those that a mesh axis runs over, the one named last changes fastest.
Arguments:
- receiver_data: bfloat16 [4, 2, 1024, 4096], P(None, None, None, 'xline'), may hold values from -6 to 6
- source_amp: bfloat16 [4, 2, 256], replicated, may hold values from -6 to 6
- source_x: int32 [256], replicated, may hold values from 0 to 1023
- source_y: int32 [256], replicated, may hold values from 0 to 4095
- omegas: float32 [4], replicated, may hold values from 0.5 to 3
- slowness: float32 [4, 1024, 4096], P('depth', None, 'xline'), may hold values from 0.2 to 2
- inverses: bfloat16 [4, 4, 2, 256, 256], replicated, may hold values from -0.1875 to 0.1875
- zones_x: int32 [4, 4], P('depth'), may hold values from 0 to 3
- zones_y: int32 [4, 16], P('depth'), may hold values from 0 to 3
Outputs:
- gradient: float32 [4, 1024, 4096], P('depth', None, 'xline')
The draws below stay inside these ranges and needn't reach their ends.
All inputs are finite; a program needn't handle non-finite values.
Results may differ from the reference program's by a relative error of at most 0.015.
Values may be sent and summed in bfloat16 or wider, within the bound.
No kernel may reach another device: no remote copies, remote signals or barrier semaphores. Data moves between devices by JAX's collectives and lax.ppermute only.
A program may use at most 64 MiB of HBM per device.

```python
import math
import jax
import jax.numpy as jnp

NX = 1024
B = 256
NF = 4
ZONES = 4
NSRC = 256
NY = 4096
NZ = 4
NXB = 4
NYB = 16


def set_ends(drawn, key, low, high):
    spot = [jax.random.randint(jax.random.fold_in(key, axis), (), 0, length) for axis, length in enumerate(drawn.shape)]
    longest = drawn.shape.index(max(drawn.shape))
    neighbour = spot[:longest] + [(spot[longest] + 1) % drawn.shape[longest]] + spot[longest + 1:]
    return drawn.at[tuple(spot)].set(low).at[tuple(neighbour)].set(high)


def block_scale(stream_key, extent, split, low, top_value):
    loudness, own = 1.0, jax.random.fold_in(stream_key, 6)
    for dim, blocks in split:
        heights = jnp.exp(jax.random.uniform(jax.random.fold_in(own, dim), (blocks,), jnp.float32, low / len(split), top_value / len(split)))
        loudness = loudness * jnp.repeat(heights, extent[dim] // blocks).reshape([-1 if axis == dim else 1 for axis in range(len(extent))])
    return loudness


def bell_draw(key, dims, scale, reach, cuts=(), dtype=jnp.bfloat16):
    array = jax.random.normal(key, dims, jnp.float32) * scale
    if len(cuts) > 0:
        array = block_scale(key, dims, cuts, -0.22, 0.18) * array
    return jnp.clip(array, min=-reach, max=reach).astype(dtype)


def setup_inputs(seed: int = 0) -> dict:
    splits = jax.random.split(jax.random.key(seed), 10)
    receiver_data = bell_draw(splits[0], (NF, 2, NX, NY), 1.0, 6.0, ((3, 32),))
    source_amp = bell_draw(splits[1], (NF, 2, NSRC), 1.0, 6.0)
    source_x = set_ends(jax.random.randint(splits[2], (NSRC,), 0, NX), jax.random.fold_in(splits[2], 1), 0, NX - 1).astype(jnp.int32)
    source_y = set_ends(jax.random.randint(splits[3], (NSRC,), 0, NY), jax.random.fold_in(splits[3], 1), 0, NY - 1).astype(jnp.int32)
    omegas = jnp.clip(jnp.exp(jax.random.uniform(splits[4], (NF,), jnp.float32, math.log(0.5), math.log(3.0))), 0.5, 3.0)
    slowness = jnp.clip(0.2 + 1.8 * jax.random.uniform(splits[5], (NZ, NX, NY), jnp.float32) ** block_scale(splits[5], (NZ, NX, NY), ((0, 4), (2, 32)), -0.2, 0.2), 0.2, 2.0)
    inverses = bell_draw(splits[6], (NF, ZONES, 2, B, B), (4 * B) ** -0.5, 0.1875)
    zones_x = set_ends(jax.random.randint(splits[7], (NZ, NXB), 0, ZONES), jax.random.fold_in(splits[7], 1), 0, ZONES - 1).astype(jnp.int32)
    zones_y = set_ends(jax.random.randint(splits[8], (NZ, NYB), 0, ZONES), jax.random.fold_in(splits[8], 1), 0, ZONES - 1).astype(jnp.int32)
    return {"receiver_data": receiver_data, "source_amp": source_amp, "source_x": source_x, "source_y": source_y, "omegas": omegas, "slowness": slowness, "inverses": inverses, "zones_x": zones_x, "zones_y": zones_y}


def rotate(field, angle, sign):
    field_real = field[0].astype(jnp.float32)
    field_imag = field[1].astype(jnp.float32)
    cosine = jnp.cos(angle)
    sine = jnp.sin(angle) * sign
    return jnp.stack([field_real * cosine - field_imag * sine, field_real * sine + field_imag * cosine]).astype(jnp.bfloat16)


def solve_inline(field, blocks, sign):
    parts = field.astype(jnp.float32).reshape(2, NX // B, B, field.shape[2])
    k_real = blocks[:, 0].astype(jnp.float32)
    k_imag = sign * blocks[:, 1].astype(jnp.float32)
    def blockwise(matrix, vector):
        return jnp.einsum("bij,bjy->biy", matrix, vector)
    out_real = parts[0] + blockwise(k_real, parts[0]) - blockwise(k_imag, parts[1])
    out_imag = parts[1] + blockwise(k_real, parts[1]) + blockwise(k_imag, parts[0])
    return jnp.stack([out_real, out_imag]).reshape(field.shape).astype(jnp.bfloat16)


def solve_crossline(field, blocks, sign):
    parts = field.astype(jnp.float32).reshape(2, field.shape[1], NY // B, B)
    k_real = blocks[:, 0].astype(jnp.float32)
    k_imag = sign * blocks[:, 1].astype(jnp.float32)
    def blockwise(matrix, vector):
        return jnp.einsum("bij,xbj->xbi", matrix, vector)
    out_real = parts[0] + blockwise(k_real, parts[0]) - blockwise(k_imag, parts[1])
    out_imag = parts[1] + blockwise(k_real, parts[1]) + blockwise(k_imag, parts[0])
    return jnp.stack([out_real, out_imag]).reshape(field.shape).astype(jnp.bfloat16)


def continue_level(field, angle, table, zone_row_x, zone_row_y, sign):
    rotated = rotate(field, angle, sign)
    inline = solve_inline(rotated, jnp.take(table, zone_row_x, axis=0), sign)
    return solve_crossline(inline, jnp.take(table, zone_row_y, axis=0), sign)


def reference(receiver_data, source_amp, source_x, source_y, omegas, slowness, inverses, zones_x, zones_y):
    source_all = jnp.zeros((NF, 2, NX, NY), jnp.float32).at[:, :, source_x, source_y].add(source_amp.astype(jnp.float32))
    source_all = source_all.astype(jnp.bfloat16)
    gradient = jnp.zeros((NZ, NX, NY), jnp.float32)
    for freq in range(NF):
        source_field = source_all[freq]
        receiver_field = receiver_data[freq]
        weight = omegas[freq] * omegas[freq]
        for level in range(NZ):
            angle = omegas[freq] * slowness[level]
            source_field = continue_level(source_field, angle, inverses[freq], zones_x[level], zones_y[level], 1.0)
            receiver_field = continue_level(receiver_field, angle, inverses[freq], zones_x[level], zones_y[level], -1.0)
            correlation = source_field[0].astype(jnp.float32) * receiver_field[0].astype(jnp.float32) + source_field[1].astype(jnp.float32) * receiver_field[1].astype(jnp.float32)
            gradient = gradient.at[level].add(weight * correlation)
    return gradient
```

```python
import math

import jax
import jax.numpy as jnp
from jax import lax
from jax.experimental import pallas as pl
from jax.experimental.pallas import tpu as pltpu
from jax.sharding import PartitionSpec as P

F32 = jnp.float32
BF16 = jnp.bfloat16
I32 = jnp.int32
I16 = jnp.int16

SECTIONS = 4
LEVELS = 4
FREQS = 4
MINE = 2
B = 256
H = 128
EXTRA = 16

MIDDLE = 1.1
STEPS = 36000.0

SIN = (4.4428679, -7.30744341, 3.59478797, -0.78437374)
COS = (1.4142135, -6.97885099, 5.73946117, -1.88356295, 0.3106981)

MB = 1 << 20


def horner(u, coefs):
    total = coefs[-1]
    for c in coefs[-2::-1]:
        total = total * u + c
    return total


def place():
    line = lax.axis_index("xline")
    return lax.axis_index("depth"), line // 2, lax.rem(line, 2)


def pack_kernel(slow, zones_x, zones_y, receiver, q0, q1, q2, q3, rec_own, rec_send, sems):
    section, pair, core = place()
    rows = pl.ds(section * B, B)
    copies = [
        pltpu.make_async_copy(
            receiver.at[pl.ds(which * MINE, MINE), :, rows, :], out, sems.at[k]
        )
        for k, (which, out) in enumerate(((1 - core, rec_send), (core, rec_own)))
    ]
    for copy in copies:
        copy.start()
    zone_y = zones_y[0, pair]
    upper = lax.broadcasted_iota(I32, (EXTRA, H), 0) < EXTRA // 2
    for shift, q in enumerate((q0, q1, q2, q3)):
        to = lax.rem(section + shift, SECTIONS)
        start = pl.multiple_of(to * B, B)
        for r in range(0, B, 32):
            value = slow[0, pl.ds(start + r, 32), :]
            level = jnp.clip((value - MIDDLE) * STEPS, -32767.0, 32767.0)
            q[r : r + 32, :] = jnp.round(level).astype(I32).astype(I16)
        q[B:, :] = jnp.where(upper, zones_x[0, to], zone_y).astype(I16)
    for copy in copies:
        copy.wait()


def pack(slowness, zones_x, zones_y, receiver):
    block = jax.ShapeDtypeStruct((B + EXTRA, H), I16)
    part = jax.ShapeDtypeStruct((MINE, 2, B, H), BF16)
    vmem = pl.BlockSpec(memory_space=pltpu.VMEM)
    smem = pl.BlockSpec(memory_space=pltpu.SMEM)
    hbm = pl.BlockSpec(memory_space=pl.ANY)
    return pl.pallas_call(
        pack_kernel,
        out_shape=[block] * 4 + [part] * 2,
        in_specs=[vmem, smem, smem, hbm],
        out_specs=[vmem] * 4 + [hbm] * 2,
        scratch_shapes=[pltpu.SemaphoreType.DMA((2,))],
        name="pack",
    )(slowness, zones_x, zones_y, receiver)


def prepare_kernel(amp, source_x, source_y, inverses, sources, operators, table, spread, sem):
    section, pair, core = place()
    copy = pltpu.make_async_copy(inverses.at[pl.ds(core * MINE, MINE)], table, sem)
    copy.start()
    count = source_x.shape[1]
    cells = lax.broadcasted_iota(I32, (B, count), 0)
    hot_x = jnp.where(cells + section * B == source_x[...], 1.0, 0.0).astype(BF16)
    hot_y = cells + pair * B == source_y[...]
    for f in range(MINE):
        for part in range(2):
            row = amp[pl.ds(core * MINE + f, 1), part, :].astype(F32)
            spread[part * B : (part + 1) * B, :] = jnp.where(hot_y, row, 0.0).astype(BF16)
        sources[f] = lax.dot_general(
            hot_x, spread[...], (((1,), (1,)), ((), ())), preferred_element_type=F32
        ).astype(BF16)
    copy.wait()
    for f in range(MINE):
        for zone in range(table.shape[1]):
            real = table[f, zone, 0]
            imag = table[f, zone, 1]
            operators[f, zone, :B, :B] = real
            operators[f, zone, B:, B:] = real
            operators[f, zone, B:, :B] = imag
            operators[f, zone, :B, B:] = -imag


def prepare(amp, source_x, source_y, inverses):
    zones = inverses.shape[1]
    vmem = pl.BlockSpec(memory_space=pltpu.VMEM)
    hbm = pl.BlockSpec(memory_space=pl.ANY)
    return pl.pallas_call(
        prepare_kernel,
        out_shape=[
            jax.ShapeDtypeStruct((MINE, B, 2 * B), BF16),
            jax.ShapeDtypeStruct((MINE, zones, 2 * B, 2 * B), BF16),
        ],
        in_specs=[vmem, vmem, vmem, hbm],
        out_specs=[vmem, vmem],
        scratch_shapes=[
            pltpu.VMEM((MINE, zones, 2, B, B), BF16),
            pltpu.VMEM((2 * B, source_x.shape[1]), BF16),
            pltpu.SemaphoreType.DMA,
        ],
        compiler_params=pltpu.CompilerParams(vmem_limit_bytes=24 * MB),
        cost_estimate=pl.CostEstimate(
            flops=4 * B**3 * 4, bytes_accessed=8 * MB, transcendentals=0
        ),
        name="prepare",
    )(amp, source_x, source_y, inverses)


def continue_kernel(
    omegas, sources, operators, rec_mine, rec_other,
    q0, q1, q2, q3, p0, p1, p2, p3,
    grad_mine, grad_other,
    slow, zones, W, X, Y,
):
    section, _, core = place()
    mine = pl.ds(pl.multiple_of(core * H, H), H)
    other = pl.ds(pl.multiple_of((1 - core) * H, H), H)

    for shift, (q, p) in enumerate(((q0, p0), (q1, p1), (q2, p2), (q3, p3))):
        level = lax.rem(section + SECTIONS - shift, SECTIONS)
        for r in range(0, B, 32):
            slow[level, r : r + 32, mine] = q[r : r + 32, :].astype(I32).astype(F32)
            slow[level, r : r + 32, other] = p[r : r + 32, :].astype(I32).astype(F32)
        marks = q[B:, :].astype(I32)
        zones[level, 0] = jnp.max(marks[: EXTRA // 2])
        zones[level, 1] = jnp.max(marks[EXTRA // 2 :])

    for f in range(MINE):
        W[f, :B, :] = sources[f]
        for columns, rec in ((mine, rec_mine), (other, rec_other)):
            W[f, B:, columns] = rec[f, 0]
        imag_mine = pl.ds(pl.multiple_of(B + core * H, H), H)
        imag_other = pl.ds(pl.multiple_of(B + (1 - core) * H, H), H)
        for columns, rec in ((imag_mine, rec_mine), (imag_other, rec_other)):
            W[f, B:, columns] = -rec[f, 1]

    def one_level(level, carry):
        zone_x = zones[level, 0]
        zone_y = zones[level, 1]
        for f in range(MINE):
            omega = omegas[core * MINE + f]
            scale = omega * (0.5 / math.pi / STEPS)
            base = omega * (0.5 / math.pi * MIDDLE) - 0.5
            for c in range(0, B, H):
                for r in range(0, B, 32):
                    turn = slow[level, r : r + 32, c : c + H] * scale + base
                    square = turn * turn
                    half_sin = turn * horner(square, SIN)
                    half_cos = horner(square, COS)
                    cosine = half_sin * half_sin - 1.0
                    sine = -half_sin * half_cos
                    for wave in range(0, 2 * B, B):
                        real = W[f, wave + r : wave + r + 32, c : c + H].astype(F32)
                        imag = W[f, wave + r : wave + r + 32, B + c : B + c + H].astype(F32)
                        X[f, r : r + 32, wave + c : wave + c + H] = (
                            real * cosine - imag * sine
                        ).astype(BF16)
                        X[f, B + r : B + r + 32, wave + c : wave + c + H] = (
                            real * sine + imag * cosine
                        ).astype(BF16)
        for f in range(MINE):
            for wave in range(0, 2 * B, B):
                update = jnp.dot(
                    operators[f, zone_x], X[f, :, wave : wave + B], preferred_element_type=F32
                )
                for part in range(0, 2 * B, B):
                    Y[f, wave : wave + B, part : part + B] = (
                        X[f, part : part + B, wave : wave + B].astype(F32)
                        + update[part : part + B]
                    ).astype(BF16)
        for f in range(MINE):
            for part in range(0, 2 * B, B):
                update = lax.dot_general(
                    Y[f],
                    operators[f, zone_y, part : part + B, :],
                    (((1,), (1,)), ((), ())),
                    preferred_element_type=F32,
                )
                W[f, :, part : part + B] = (
                    Y[f, :, part : part + B].astype(F32) + update
                ).astype(BF16)
        for out, offset in ((grad_mine, core * H), (grad_other, (1 - core) * H)):
            real_at = pl.ds(pl.multiple_of(offset, H), H)
            imag_at = pl.ds(pl.multiple_of(B + offset, H), H)
            for r in range(0, B, 32):
                total = None
                for f in range(MINE):
                    omega = omegas[core * MINE + f]
                    down = slice(r, r + 32)
                    up = slice(B + r, B + r + 32)
                    term = W[f, down, real_at].astype(F32) * W[f, up, real_at].astype(F32)
                    term -= W[f, down, imag_at].astype(F32) * W[f, up, imag_at].astype(F32)
                    term *= omega * omega
                    total = term if total is None else total + term
                out[level, r : r + 32, :] = total.astype(out.dtype)
        return carry

    lax.fori_loop(0, LEVELS, one_level, 0)


def continue_all(omegas, sources, operators, rec_mine, rec_other, mine, other):
    vmem = pl.BlockSpec(memory_space=pltpu.VMEM)
    smem = pl.BlockSpec(memory_space=pltpu.SMEM)
    return pl.pallas_call(
        continue_kernel,
        out_shape=[
            jax.ShapeDtypeStruct((LEVELS, B, H), F32),
            jax.ShapeDtypeStruct((LEVELS, B, H), BF16),
        ],
        in_specs=[smem] + [vmem] * 12,
        out_specs=[vmem, vmem],
        scratch_shapes=[
            pltpu.VMEM((LEVELS, B, B), F32),
            pltpu.SMEM((LEVELS, 2), I32),
            pltpu.VMEM((MINE, 2 * B, 2 * B), BF16),
            pltpu.VMEM((MINE, 2 * B, 2 * B), BF16),
            pltpu.VMEM((MINE, 2 * B, 2 * B), BF16),
        ],
        compiler_params=pltpu.CompilerParams(vmem_limit_bytes=32 * MB),
        cost_estimate=pl.CostEstimate(
            flops=2 * 128 * B**3, bytes_accessed=8 * MB, transcendentals=0
        ),
        name="continue_levels",
    )(omegas, sources, operators, rec_mine, rec_other, *mine, *other)


def merge_kernel(mine, got, own, s1, s2, s3):
    section, _, _ = place()
    for shift, out in enumerate((own, s1, s2, s3)):
        level = lax.rem(section + shift, SECTIONS)
        out[...] = (mine[level] + got[level].astype(F32)).astype(out.dtype)


def merge(mine, got):
    vmem = pl.BlockSpec(memory_space=pltpu.VMEM)
    return pl.pallas_call(
        merge_kernel,
        out_shape=[jax.ShapeDtypeStruct((B, H), F32)]
        + [jax.ShapeDtypeStruct((B, H), BF16)] * 3,
        in_specs=[vmem, vmem],
        out_specs=[vmem] * 4,
        name="merge",
    )(mine, got)


def assemble_kernel(own, g1, g2, g3, out):
    section, _, _ = place()
    for shift, block in enumerate((own, g1, g2, g3)):
        origin = lax.rem(section + SECTIONS - shift, SECTIONS)
        out[0, pl.ds(pl.multiple_of(origin * B, B), B), :] = block[...].astype(F32)


def assemble(own, blocks):
    vmem = pl.BlockSpec(memory_space=pltpu.VMEM)
    return pl.pallas_call(
        assemble_kernel,
        out_shape=jax.ShapeDtypeStruct((1, SECTIONS * B, H), F32),
        in_specs=[vmem] * 4,
        out_specs=vmem,
        name="assemble",
    )(own, *blocks)


def along_depth(block, shift):
    return lax.ppermute(block, "depth", [(i, (i + shift) % SECTIONS) for i in range(SECTIONS)])


def other_core(block):
    count = lax.axis_size("xline")
    return lax.ppermute(block, "xline", [(i, i ^ 1) for i in range(count)])


def per_device(
    receiver_data, source_amp, source_x, source_y, omegas, slowness, inverses, zones_x, zones_y
):
    *blocks, rec_mine, rec_send = pack(slowness, zones_x, zones_y, receiver_data)
    mine = [blocks[0]] + [along_depth(blocks[k], k) for k in (1, 2, 3)]
    other = [other_core(block) for block in mine]
    rec_other = other_core(rec_send)
    sources, operators = prepare(
        source_amp, source_x.reshape(1, -1), source_y.reshape(1, -1), inverses
    )
    grad_mine, grad_other = continue_all(
        omegas, sources, operators, rec_mine, rec_other, mine, other
    )
    own, *parts = merge(grad_mine, other_core(grad_other))
    return assemble(own, [along_depth(parts[k - 1], k) for k in (1, 2, 3)])


def solution(mesh):
    in_specs = (
        P(None, None, None, "xline"),
        P(),
        P(),
        P(),
        P(),
        P("depth", None, "xline"),
        P(),
        P("depth", None),
        P("depth", None),
    )
    return jax.shard_map(
        per_device,
        mesh=mesh,
        in_specs=in_specs,
        out_specs=P("depth", None, "xline"),
        check_vma=False,
    )
```

```python
import math

import jax
import jax.numpy as jnp
from jax import lax
from jax.experimental import pallas as pl
from jax.experimental.pallas import tpu as pltpu
from jax.sharding import PartitionSpec as P

F32 = jnp.float32
BF16 = jnp.bfloat16
I32 = jnp.int32
I16 = jnp.int16

SECTIONS = 4
LEVELS = 4
FREQS = 4
MINE = 2
B = 256
H = 128
EXTRA = 16

MIDDLE = 1.1
STEPS = 36000.0

SIN = (4.4428679, -7.30744341, 3.59478797, -0.78437374)
COS = (1.4142135, -6.97885099, 5.73946117, -1.88356295, 0.3106981)

MB = 1 << 20


def horner(u, coefs):
    total = coefs[-1]
    for c in coefs[-2::-1]:
        total = total * u + c
    return total


def place():
    line = lax.axis_index("xline")
    return lax.axis_index("depth"), line // 2, lax.rem(line, 2)


def pack_kernel(
    slow, zones_x, zones_y, receiver, amp_hbm, source_x_hbm, source_y_hbm,
    q0, q1, q2, q3, rec_mine, rec_send, sources,
    level_slow, packed, rec, amp, source_x, source_y, spread, fields, in_sems, out_sems,
):
    section, pair, core = place()
    order = ((1, q1), (2, q2), (3, q3), (0, q0))
    rows = pl.ds(pl.multiple_of(section * B, B), B)
    arrivals = []
    for shift, _ in order:
        to = lax.rem(section + shift, SECTIONS)
        start = pl.ds(pl.multiple_of(to * B, B), B)
        arrivals.append((slow.at[0, start, :], level_slow.at[shift]))
    arrivals += [(amp_hbm, amp), (source_x_hbm, source_x), (source_y_hbm, source_y)]
    for k in range(2):
        freqs = pl.ds(lax.rem(core + k, 2) * MINE, MINE)
        arrivals.append((receiver.at[freqs, :, rows, :], rec.at[k]))
    arrivals = [pltpu.make_async_copy(*ends, in_sems.at[k]) for k, ends in enumerate(arrivals)]
    for copy in arrivals:
        copy.start()

    departures = []

    def send(source, target):
        copy = pltpu.make_async_copy(source, target, out_sems.at[len(departures)])
        copy.start()
        departures.append(copy)

    zone_y = zones_y[0, pair]
    upper = lax.broadcasted_iota(I32, (EXTRA, H), 0) < EXTRA // 2
    for (shift, q), copy in zip(order, arrivals):
        to = lax.rem(section + shift, SECTIONS)
        packed[shift, B:, :] = jnp.where(upper, zones_x[0, to], zone_y).astype(I16)
        copy.wait()
        for r in range(0, B, 32):
            level = (level_slow[shift, r : r + 32, :] - MIDDLE) * STEPS
            level = jnp.clip(level, -32767.0, 32767.0)
            packed[shift, r : r + 32, :] = jnp.round(level).astype(I32).astype(I16)
        send(packed.at[shift], q)
    for copy in arrivals[SECTIONS:]:
        copy.wait()
    send(rec.at[1], rec_send)
    send(rec.at[0], rec_mine)

    count = source_x.shape[1]
    cells = lax.broadcasted_iota(I32, (B, count), 0)
    hot_x = jnp.where(cells + section * B == source_x[...], 1.0, 0.0).astype(BF16)
    hot_y = cells + pair * B == source_y[...]
    for f in range(MINE):
        for part in range(2):
            row = amp[pl.ds(core * MINE + f, 1), part, :].astype(F32)
            spread[part * B : (part + 1) * B, :] = jnp.where(hot_y, row, 0.0).astype(BF16)
        fields[f] = lax.dot_general(
            hot_x, spread[...], (((1,), (1,)), ((), ())), preferred_element_type=F32
        ).astype(BF16)
    send(fields, sources)
    for copy in departures:
        copy.wait()


def pack(slowness, zones_x, zones_y, receiver, amp, source_x, source_y):
    block = jax.ShapeDtypeStruct((B + EXTRA, H), I16)
    part = jax.ShapeDtypeStruct((MINE, 2, B, H), BF16)
    field = jax.ShapeDtypeStruct((MINE, B, 2 * B), BF16)
    smem = pl.BlockSpec(memory_space=pltpu.SMEM)
    hbm = pl.BlockSpec(memory_space=pl.ANY)
    return pl.pallas_call(
        pack_kernel,
        out_shape=[block] * 4 + [part] * 2 + [field],
        in_specs=[hbm, smem, smem] + [hbm] * 4,
        out_specs=[hbm] * 7,
        scratch_shapes=[
            pltpu.VMEM((SECTIONS, B, H), F32),
            pltpu.VMEM((SECTIONS, B + EXTRA, H), I16),
            pltpu.VMEM((2, MINE, 2, B, H), BF16),
            pltpu.VMEM(amp.shape, BF16),
            pltpu.VMEM(source_x.shape, I32),
            pltpu.VMEM(source_y.shape, I32),
            pltpu.VMEM((2 * B, source_x.shape[1]), BF16),
            pltpu.VMEM((MINE, B, 2 * B), BF16),
            pltpu.SemaphoreType.DMA((9,)),
            pltpu.SemaphoreType.DMA((7,)),
        ],
        name="pack",
    )(slowness, zones_x, zones_y, receiver, amp, source_x, source_y)


def prepare_kernel(inverses, operators, table, sems):
    core = place()[2]
    copies = [
        pltpu.make_async_copy(inverses.at[core * MINE + f], table.at[f], sems.at[f])
        for f in range(MINE)
    ]
    for copy in copies:
        copy.start()
    for f in range(MINE):
        copies[f].wait()
        for zone in range(table.shape[1]):
            real = table[f, zone, 0]
            imag = table[f, zone, 1]
            operators[f, zone, :B, :B] = real
            operators[f, zone, B:, B:] = real
            operators[f, zone, B:, :B] = imag
            operators[f, zone, :B, B:] = -imag


def prepare(inverses):
    zones = inverses.shape[1]
    return pl.pallas_call(
        prepare_kernel,
        out_shape=jax.ShapeDtypeStruct((MINE, zones, 2 * B, 2 * B), BF16),
        in_specs=[pl.BlockSpec(memory_space=pltpu.HBM)],
        out_specs=pl.BlockSpec(memory_space=pltpu.VMEM),
        scratch_shapes=[
            pltpu.VMEM((MINE, zones, 2, B, B), BF16),
            pltpu.SemaphoreType.DMA((MINE,)),
        ],
        compiler_params=pltpu.CompilerParams(vmem_limit_bytes=48 * MB),
        cost_estimate=pl.CostEstimate(flops=0, bytes_accessed=6 * MB, transcendentals=0),
        name="prepare",
    )(inverses)


def continue_kernel(
    omegas, sources, operators, rec_mine, rec_other,
    q0, q1, q2, q3, p0, p1, p2, p3,
    grad_mine, grad_other,
    slow, zones, W, X, Y,
):
    section, _, core = place()
    mine = pl.ds(pl.multiple_of(core * H, H), H)
    other = pl.ds(pl.multiple_of((1 - core) * H, H), H)

    for shift, (q, p) in enumerate(((q0, p0), (q1, p1), (q2, p2), (q3, p3))):
        level = lax.rem(section + SECTIONS - shift, SECTIONS)
        for r in range(0, B, 32):
            slow[level, r : r + 32, mine] = q[r : r + 32, :].astype(I32).astype(F32)
            slow[level, r : r + 32, other] = p[r : r + 32, :].astype(I32).astype(F32)
        marks = q[B:, :].astype(I32)
        zones[level, 0] = jnp.max(marks[: EXTRA // 2])
        zones[level, 1] = jnp.max(marks[EXTRA // 2 :])

    for f in range(MINE):
        W[f, :B, :] = sources[f]
        for columns, rec in ((mine, rec_mine), (other, rec_other)):
            W[f, B:, columns] = rec[f, 0]
        imag_mine = pl.ds(pl.multiple_of(B + core * H, H), H)
        imag_other = pl.ds(pl.multiple_of(B + (1 - core) * H, H), H)
        for columns, rec in ((imag_mine, rec_mine), (imag_other, rec_other)):
            W[f, B:, columns] = -rec[f, 1]

    def one_level(level, carry):
        zone_x = zones[level, 0]
        zone_y = zones[level, 1]
        for f in range(MINE):
            omega = omegas[core * MINE + f]
            scale = omega * (0.5 / math.pi / STEPS)
            base = omega * (0.5 / math.pi * MIDDLE) - 0.5
            for c in range(0, B, H):
                for r in range(0, B, 32):
                    turn = slow[level, r : r + 32, c : c + H] * scale + base
                    square = turn * turn
                    half_sin = turn * horner(square, SIN)
                    half_cos = horner(square, COS)
                    cosine = half_sin * half_sin - 1.0
                    sine = -half_sin * half_cos
                    for wave in range(0, 2 * B, B):
                        real = W[f, wave + r : wave + r + 32, c : c + H].astype(F32)
                        imag = W[f, wave + r : wave + r + 32, B + c : B + c + H].astype(F32)
                        X[f, r : r + 32, wave + c : wave + c + H] = (
                            real * cosine - imag * sine
                        ).astype(BF16)
                        X[f, B + r : B + r + 32, wave + c : wave + c + H] = (
                            real * sine + imag * cosine
                        ).astype(BF16)
        for f in range(MINE):
            for wave in range(0, 2 * B, B):
                update = jnp.dot(
                    operators[f, zone_x], X[f, :, wave : wave + B], preferred_element_type=F32
                )
                for part in range(0, 2 * B, B):
                    Y[f, wave : wave + B, part : part + B] = (
                        X[f, part : part + B, wave : wave + B].astype(F32)
                        + update[part : part + B]
                    ).astype(BF16)
        for f in range(MINE):
            for part in range(0, 2 * B, B):
                update = lax.dot_general(
                    Y[f],
                    operators[f, zone_y, part : part + B, :],
                    (((1,), (1,)), ((), ())),
                    preferred_element_type=F32,
                )
                W[f, :, part : part + B] = (
                    Y[f, :, part : part + B].astype(F32) + update
                ).astype(BF16)
        for out, offset in ((grad_mine, core * H), (grad_other, (1 - core) * H)):
            real_at = pl.ds(pl.multiple_of(offset, H), H)
            imag_at = pl.ds(pl.multiple_of(B + offset, H), H)
            for r in range(0, B, 32):
                total = None
                for f in range(MINE):
                    omega = omegas[core * MINE + f]
                    down = slice(r, r + 32)
                    up = slice(B + r, B + r + 32)
                    term = W[f, down, real_at].astype(F32) * W[f, up, real_at].astype(F32)
                    term -= W[f, down, imag_at].astype(F32) * W[f, up, imag_at].astype(F32)
                    term *= omega * omega
                    total = term if total is None else total + term
                out[level, r : r + 32, :] = total.astype(out.dtype)
        return carry

    lax.fori_loop(0, LEVELS, one_level, 0)


def continue_all(omegas, sources, operators, rec_mine, rec_other, mine, other):
    vmem = pl.BlockSpec(memory_space=pltpu.VMEM)
    smem = pl.BlockSpec(memory_space=pltpu.SMEM)
    return pl.pallas_call(
        continue_kernel,
        out_shape=[
            jax.ShapeDtypeStruct((LEVELS, B, H), F32),
            jax.ShapeDtypeStruct((LEVELS, B, H), BF16),
        ],
        in_specs=[smem] + [vmem] * 12,
        out_specs=[vmem, vmem],
        scratch_shapes=[
            pltpu.VMEM((LEVELS, B, B), F32),
            pltpu.SMEM((LEVELS, 2), I32),
            pltpu.VMEM((MINE, 2 * B, 2 * B), BF16),
            pltpu.VMEM((MINE, 2 * B, 2 * B), BF16),
            pltpu.VMEM((MINE, 2 * B, 2 * B), BF16),
        ],
        compiler_params=pltpu.CompilerParams(vmem_limit_bytes=32 * MB),
        cost_estimate=pl.CostEstimate(
            flops=2 * 128 * B**3, bytes_accessed=8 * MB, transcendentals=0
        ),
        name="continue_levels",
    )(omegas, sources, operators, rec_mine, rec_other, *mine, *other)


def merge_kernel(mine, got, own, s1, s2, s3):
    section, _, _ = place()
    for shift, out in enumerate((own, s1, s2, s3)):
        level = lax.rem(section + shift, SECTIONS)
        out[...] = (mine[level] + got[level].astype(F32)).astype(out.dtype)


def merge(mine, got):
    vmem = pl.BlockSpec(memory_space=pltpu.VMEM)
    return pl.pallas_call(
        merge_kernel,
        out_shape=[jax.ShapeDtypeStruct((B, H), F32)]
        + [jax.ShapeDtypeStruct((B, H), BF16)] * 3,
        in_specs=[vmem, vmem],
        out_specs=[vmem] * 4,
        compiler_params=pltpu.CompilerParams(vmem_limit_bytes=8 * MB),
        name="merge",
    )(mine, got)


def assemble_kernel(own, g1, g2, g3, out):
    section, _, _ = place()
    for shift, block in enumerate((own, g1, g2, g3)):
        origin = lax.rem(section + SECTIONS - shift, SECTIONS)
        out[0, pl.ds(pl.multiple_of(origin * B, B), B), :] = block[...].astype(F32)


def assemble(own, blocks):
    vmem = pl.BlockSpec(memory_space=pltpu.VMEM)
    return pl.pallas_call(
        assemble_kernel,
        out_shape=jax.ShapeDtypeStruct((1, SECTIONS * B, H), F32),
        in_specs=[vmem] * 4,
        out_specs=vmem,
        compiler_params=pltpu.CompilerParams(vmem_limit_bytes=8 * MB),
        name="assemble",
    )(own, *blocks)


def along_depth(block, shift):
    return lax.ppermute(block, "depth", [(i, (i + shift) % SECTIONS) for i in range(SECTIONS)])


def other_core(block):
    count = lax.axis_size("xline")
    return lax.ppermute(block, "xline", [(i, i ^ 1) for i in range(count)])


def per_device(
    receiver_data, source_amp, source_x, source_y, omegas, slowness, inverses, zones_x, zones_y
):
    *blocks, rec_mine, rec_send, sources = pack(
        slowness,
        zones_x,
        zones_y,
        receiver_data,
        source_amp,
        source_x.reshape(1, -1),
        source_y.reshape(1, -1),
    )
    moved = [along_depth(blocks[k], k) for k in (1, 2, 3)]
    operators = prepare(inverses)
    operators, rec_send, own, *moved = lax.optimization_barrier(
        (operators, rec_send, blocks[0], *moved)
    )
    mine = [own, *moved]
    rec_other = other_core(rec_send)
    other = [other_core(block) for block in mine]
    grad_mine, grad_other = continue_all(
        omegas, sources, operators, rec_mine, rec_other, mine, other
    )
    own, *parts = merge(grad_mine, other_core(grad_other))
    return assemble(own, [along_depth(parts[k - 1], k) for k in (1, 2, 3)])


def solution(mesh):
    in_specs = (
        P(None, None, None, "xline"),
        P(),
        P(),
        P(),
        P(),
        P("depth", None, "xline"),
        P(),
        P("depth", None),
        P("depth", None),
    )
    return jax.shard_map(
        per_device,
        mesh=mesh,
        in_specs=in_specs,
        out_specs=P("depth", None, "xline"),
        check_vma=False,
    )
```

```python
import math

import jax
import jax.numpy as jnp
from jax import lax
from jax.experimental import pallas as pl
from jax.experimental.pallas import tpu as pltpu
from jax.sharding import PartitionSpec as P

F32 = jnp.float32
BF16 = jnp.bfloat16
I32 = jnp.int32
I16 = jnp.int16

SECTIONS = 4
LEVELS = 4
FREQS = 4
MINE = 2
B = 256
H = 128
EBF16RA = 16

MIDDLE = 1.1
STEPS = 36000.0

SIN = (4.4428679, -7.30744341, 3.59478797, -0.78437374)
COS = (1.4142135, -6.97885099, 5.73946117, -1.88356295, 0.3106981)

MB = 1 << 20


def horner(u, coefs):
    total = coefs[-1]
    for c in coefs[-2::-1]:
        total = total * u + c
    return total


def place():
    line = lax.axis_index("xline")
    return lax.axis_index("depth"), line // 2, lax.rem(line, 2)


def pack_kernel(
    slow, zones_x, zones_y, receiver, amp_hbm, source_x_hbm, source_y_hbm,
    q0, q1, q2, q3, rec_mine, rec_send, sources,
    level_slow, packed, rec, amp, source_x, source_y, spread, fields, in_sems, out_sems,
):
    section, pair, core = place()
    order = ((1, q1), (2, q2), (3, q3), (0, q0))
    rows = pl.ds(pl.multiple_of(section * B, B), B)
    arrivals = []
    for shift, _ in order:
        to = lax.bitwise_xor(section, shift)
        start = pl.ds(pl.multiple_of(to * B, B), B)
        arrivals.append((slow.at[0, start, :], level_slow.at[shift]))
    arrivals += [(amp_hbm, amp), (source_x_hbm, source_x), (source_y_hbm, source_y)]
    for k in range(2):
        freqs = pl.ds(lax.rem(core + k, 2) * MINE, MINE)
        arrivals.append((receiver.at[freqs, :, rows, :], rec.at[k]))
    arrivals = [pltpu.make_async_copy(*ends, in_sems.at[k]) for k, ends in enumerate(arrivals)]
    for copy in arrivals:
        copy.start()

    departures = []

    def send(source, target):
        copy = pltpu.make_async_copy(source, target, out_sems.at[len(departures)])
        copy.start()
        departures.append(copy)

    zone_y = zones_y[0, pair]
    upper = lax.broadcasted_iota(I32, (EBF16RA, H), 0) < EBF16RA // 2
    for (shift, q), copy in zip(order, arrivals):
        to = lax.bitwise_xor(section, shift)
        packed[shift, B:, :] = jnp.where(upper, zones_x[0, to], zone_y).astype(I16)
        copy.wait()
        for r in range(0, B, 32):
            level = (level_slow[shift, r : r + 32, :] - MIDDLE) * STEPS
            level = jnp.clip(level, -32767.0, 32767.0)
            packed[shift, r : r + 32, :] = jnp.round(level).astype(I32).astype(I16)
        send(packed.at[shift], q)
    for copy in arrivals[SECTIONS:]:
        copy.wait()
    send(rec.at[1], rec_send)
    send(rec.at[0], rec_mine)

    count = source_x.shape[1]
    cells = lax.broadcasted_iota(I32, (B, count), 0)
    hot_x = jnp.where(cells + section * B == source_x[...], 1.0, 0.0).astype(BF16)
    hot_y = cells + pair * B == source_y[...]
    for f in range(MINE):
        for part in range(2):
            row = amp[pl.ds(core * MINE + f, 1), part, :].astype(F32)
            spread[part * B : (part + 1) * B, :] = jnp.where(hot_y, row, 0.0).astype(BF16)
        fields[f] = lax.dot_general(
            hot_x, spread[...], (((1,), (1,)), ((), ())), preferred_element_type=F32
        ).astype(BF16)
    send(fields, sources)
    for copy in departures:
        copy.wait()


def pack(slowness, zones_x, zones_y, receiver, amp, source_x, source_y):
    block = jax.ShapeDtypeStruct((B + EBF16RA, H), I16)
    part = jax.ShapeDtypeStruct((MINE, 2, B, H), BF16)
    field = jax.ShapeDtypeStruct((MINE, B, 2 * B), BF16)
    smem = pl.BlockSpec(memory_space=pltpu.SMEM)
    hbm = pl.BlockSpec(memory_space=pl.ANY)
    return pl.pallas_call(
        pack_kernel,
        out_shape=[block] * 4 + [part] * 2 + [field],
        in_specs=[hbm, smem, smem] + [hbm] * 4,
        out_specs=[hbm] * 7,
        scratch_shapes=[
            pltpu.VMEM((SECTIONS, B, H), F32),
            pltpu.VMEM((SECTIONS, B + EBF16RA, H), I16),
            pltpu.VMEM((2, MINE, 2, B, H), BF16),
            pltpu.VMEM(amp.shape, BF16),
            pltpu.VMEM(source_x.shape, I32),
            pltpu.VMEM(source_y.shape, I32),
            pltpu.VMEM((2 * B, source_x.shape[1]), BF16),
            pltpu.VMEM((MINE, B, 2 * B), BF16),
            pltpu.SemaphoreType.DMA((9,)),
            pltpu.SemaphoreType.DMA((7,)),
        ],
        name="pack",
    )(slowness, zones_x, zones_y, receiver, amp, source_x, source_y)


def prepare_kernel(inverses, operators, table, sems):
    core = place()[2]
    copies = [
        pltpu.make_async_copy(inverses.at[core * MINE + f], table.at[f], sems.at[f])
        for f in range(MINE)
    ]
    for copy in copies:
        copy.start()
    for f in range(MINE):
        copies[f].wait()
        for zone in range(table.shape[1]):
            real = table[f, zone, 0]
            imag = table[f, zone, 1]
            operators[f, zone, :B, :B] = real
            operators[f, zone, B:, B:] = real
            operators[f, zone, B:, :B] = imag
            operators[f, zone, :B, B:] = -imag


def prepare(inverses):
    zones = inverses.shape[1]
    return pl.pallas_call(
        prepare_kernel,
        out_shape=jax.ShapeDtypeStruct((MINE, zones, 2 * B, 2 * B), BF16),
        in_specs=[pl.BlockSpec(memory_space=pltpu.HBM)],
        out_specs=pl.BlockSpec(memory_space=pltpu.VMEM),
        scratch_shapes=[
            pltpu.VMEM((MINE, zones, 2, B, B), BF16),
            pltpu.SemaphoreType.DMA((MINE,)),
        ],
        compiler_params=pltpu.CompilerParams(vmem_limit_bytes=48 * MB),
        cost_estimate=pl.CostEstimate(flops=0, bytes_accessed=6 * MB, transcendentals=0),
        name="prepare",
    )(inverses)


def continue_kernel(
    omegas, sources, operators, rec_mine, rec_other,
    q0, q1, q2, q3, p0, p1, p2, p3,
    grad_mine, grad_other,
    slow, zones, total, *waves,
):
    section, _, core = place()
    W, X, Y = waves[:MINE], waves[MINE : 2 * MINE], waves[2 * MINE :]
    mine = pl.ds(pl.multiple_of(core * H, H), H)
    other = pl.ds(pl.multiple_of((1 - core) * H, H), H)

    for shift, (q, p) in enumerate(((q0, p0), (q1, p1), (q2, p2), (q3, p3))):
        level = lax.bitwise_xor(section, shift)
        for r in range(0, B, 32):
            slow[level, r : r + 32, mine] = q[r : r + 32, :].astype(I32).astype(F32)
            slow[level, r : r + 32, other] = p[r : r + 32, :].astype(I32).astype(F32)
        marks = q[B:, :].astype(I32)
        zones[level, 0] = jnp.max(marks[: EBF16RA // 2])
        zones[level, 1] = jnp.max(marks[EBF16RA // 2 :])

    for f in range(MINE):
        W[f][:B, :] = sources[f]
        for columns, rec in ((mine, rec_mine), (other, rec_other)):
            W[f][B:, columns] = rec[f, 0]
        imag_mine = pl.ds(pl.multiple_of(B + core * H, H), H)
        imag_other = pl.ds(pl.multiple_of(B + (1 - core) * H, H), H)
        for columns, rec in ((imag_mine, rec_mine), (imag_other, rec_other)):
            W[f][B:, columns] = -rec[f, 1]

    CH = 32

    def rotate(level, f):
        omega = omegas[core * MINE + f]
        scale = omega * (0.5 / math.pi / STEPS)
        base = omega * (0.5 / math.pi * MIDDLE) - 0.5
        for c in range(0, B, H):
            for r in range(0, B, CH):
                turn = slow[level, r : r + CH, c : c + H] * scale + base
                square = turn * turn
                half_sin = turn * horner(square, SIN)
                half_cos = horner(square, COS)
                cosine = half_sin * half_sin - 1.0
                sine = -half_sin * half_cos
                for wave in range(0, 2 * B, B):
                    rows = slice(wave + r, wave + r + CH)
                    columns = slice(wave + c, wave + c + H)
                    real = W[f][rows, c : c + H].astype(F32)
                    imag = W[f][rows, B + c : B + c + H].astype(F32)
                    X[f][r : r + CH, columns] = (real * cosine - imag * sine).astype(BF16)
                    X[f][B + r : B + r + CH, columns] = (real * sine + imag * cosine).astype(BF16)

    def inline(level, f):
        zone = zones[level, 0]
        for wave in range(0, 2 * B, B):
            update = jnp.dot(
                operators[f, zone], X[f][:, wave : wave + B].astype(BF16), preferred_element_type=F32
            )
            for part in range(0, 2 * B, B):
                Y[f][wave : wave + B, part : part + B] = (
                    X[f][part : part + B, wave : wave + B].astype(F32) + update[part : part + B]
                ).astype(BF16)

    def crossline(level, f):
        zone = zones[level, 1]
        omega = omegas[core * MINE + f]
        update = lax.dot_general(
            Y[f][...], operators[f, zone], (((1,), (1,)), ((), ())), preferred_element_type=F32
        )
        for c in range(0, B, H):
            for r in range(0, B, CH):
                new = []
                for part in range(0, 2 * B, B):
                    for wave in range(0, 2 * B, B):
                        rows = slice(wave + r, wave + r + CH)
                        columns = slice(part + c, part + c + H)
                        value = Y[f][rows, columns].astype(F32) + update[rows, columns]
                        W[f][rows, columns] = value.astype(BF16)
                        new.append(value)
                term = (new[0] * new[1] - new[2] * new[3]) * (omega * omega)
                if f > 0:
                    term += total[c // H, level, r : r + CH, :]
                total[c // H, level, r : r + CH, :] = term

    def one_level(level, carry):
        for f in range(MINE):
            rotate(level, f)
        for f in range(MINE):
            inline(level, f)
        for f in range(MINE):
            crossline(level, f)
        return carry

    lax.fori_loop(0, LEVELS, one_level, 0)
    grad_mine[...] = total[core]
    grad_other[...] = total[1 - core].astype(BF16)


def continue_all(omegas, sources, operators, rec_mine, rec_other, mine, other):
    vmem = pl.BlockSpec(memory_space=pltpu.VMEM)
    smem = pl.BlockSpec(memory_space=pltpu.SMEM)
    return pl.pallas_call(
        continue_kernel,
        out_shape=[
            jax.ShapeDtypeStruct((LEVELS, B, H), F32),
            jax.ShapeDtypeStruct((LEVELS, B, H), BF16),
        ],
        in_specs=[smem] + [vmem] * 12,
        out_specs=[vmem, vmem],
        scratch_shapes=[
            pltpu.VMEM((LEVELS, B, B), F32),
            pltpu.SMEM((LEVELS, 2), I32),
            pltpu.VMEM((2, LEVELS, B, H), F32),
            *[pltpu.VMEM((2 * B, 2 * B), BF16)] * MINE,
            *[pltpu.VMEM((2 * B, 2 * B), BF16)] * MINE,
            *[pltpu.VMEM((2 * B, 2 * B), BF16)] * MINE,
        ],
        compiler_params=pltpu.CompilerParams(vmem_limit_bytes=32 * MB),
        cost_estimate=pl.CostEstimate(
            flops=2 * 128 * B**3, bytes_accessed=8 * MB, transcendentals=0
        ),
        name="continue_levels",
    )(omegas, sources, operators, rec_mine, rec_other, *mine, *other)


def merge_kernel(mine, got, own, s1, s2, s3):
    section, _, _ = place()
    for shift, out in enumerate((own, s1, s2, s3)):
        level = lax.bitwise_xor(section, shift)
        out[...] = (mine[level] + got[level].astype(F32)).astype(out.dtype)


def merge(mine, got):
    vmem = pl.BlockSpec(memory_space=pltpu.VMEM)
    return pl.pallas_call(
        merge_kernel,
        out_shape=[jax.ShapeDtypeStruct((B, H), F32)]
        + [jax.ShapeDtypeStruct((B, H), BF16)] * 3,
        in_specs=[vmem, vmem],
        out_specs=[vmem] * 4,
        compiler_params=pltpu.CompilerParams(vmem_limit_bytes=8 * MB),
        name="merge",
    )(mine, got)


def assemble_kernel(own, g1, g2, g3, out):
    section, _, _ = place()
    for shift, block in enumerate((own, g1, g2, g3)):
        origin = lax.bitwise_xor(section, shift)
        out[0, pl.ds(pl.multiple_of(origin * B, B), B), :] = block[...].astype(F32)


def assemble(own, blocks):
    vmem = pl.BlockSpec(memory_space=pltpu.VMEM)
    return pl.pallas_call(
        assemble_kernel,
        out_shape=jax.ShapeDtypeStruct((1, SECTIONS * B, H), F32),
        in_specs=[vmem] * 4,
        out_specs=vmem,
        compiler_params=pltpu.CompilerParams(vmem_limit_bytes=8 * MB),
        name="assemble",
    )(own, *blocks)


def along_depth(block, shift):
    return lax.ppermute(block, "depth", [(i, i ^ shift) for i in range(SECTIONS)])


def other_core(block):
    count = lax.axis_size("xline")
    return lax.ppermute(block, "xline", [(i, i ^ 1) for i in range(count)])


def per_device(
    receiver_data, source_amp, source_x, source_y, omegas, slowness, inverses, zones_x, zones_y
):
    *blocks, rec_mine, rec_send, sources = pack(
        slowness,
        zones_x,
        zones_y,
        receiver_data,
        source_amp,
        source_x.reshape(1, -1),
        source_y.reshape(1, -1),
    )
    moved = [along_depth(blocks[k], k) for k in (1, 2, 3)]
    rec_other = other_core(rec_send)
    own_other = other_core(blocks[0])
    operators, *moved = lax.optimization_barrier((prepare(inverses), *moved))
    mine = [blocks[0], *moved]
    other = [own_other] + [other_core(block) for block in moved]
    grad_mine, grad_other = continue_all(
        omegas, sources, operators, rec_mine, rec_other, mine, other
    )
    own, *parts = merge(grad_mine, other_core(grad_other))
    return assemble(own, [along_depth(parts[k - 1], k) for k in (1, 2, 3)])


def solution(mesh):
    in_specs = (
        P(None, None, None, "xline"),
        P(),
        P(),
        P(),
        P(),
        P("depth", None, "xline"),
        P(),
        P("depth", None),
        P("depth", None),
    )
    return jax.shard_map(
        per_device,
        mesh=mesh,
        in_specs=in_specs,
        out_specs=P("depth", None, "xline"),
        check_vma=False,
    )
```

```python
import math

import jax
import jax.numpy as jnp
from jax import lax
from jax.experimental import pallas as pl
from jax.experimental.pallas import tpu as pltpu
from jax.sharding import PartitionSpec as P

F32 = jnp.float32
BF16 = jnp.bfloat16
I32 = jnp.int32
I16 = jnp.int16

SECTIONS = 4
LEVELS = 4
FREQS = 4
MINE = 2
B = 256
H = 128
EXTRA = 16

MIDDLE = 1.1
STEPS = 36000.0

SIN = (4.4428679, -7.30744341, 3.59478797, -0.78437374)
COS = (1.4142135, -6.97885099, 5.73946117, -1.88356295, 0.3106981)

MB = 1 << 20


def horner(u, coefs):
    total = coefs[-1]
    for c in coefs[-2::-1]:
        total = total * u + c
    return total


def place():
    line = lax.axis_index("xline")
    return lax.axis_index("depth"), line // 2, lax.rem(line, 2)


def pack_kernel(slow, zones_x, zones_y, q0, q1, q2, q3, raw, packed, in_sems, out_sems):
    section, pair, _ = place()
    order = ((1, q1), (2, q2), (3, q3), (0, q0))
    arrivals = []
    for shift, _ in order:
        start = pl.ds(pl.multiple_of(lax.bitwise_xor(section, shift) * B, B), B)
        arrivals.append(
            pltpu.make_async_copy(slow.at[0, start, :], raw.at[shift], in_sems.at[shift])
        )
        arrivals[-1].start()
    zone_y = zones_y[0, pair]
    upper = lax.broadcasted_iota(I32, (EXTRA, H), 0) < EXTRA // 2
    departures = []
    for (shift, q), arrival in zip(order, arrivals):
        to = lax.bitwise_xor(section, shift)
        packed[shift, B:, :] = jnp.where(upper, zones_x[0, to], zone_y).astype(I16)
        arrival.wait()
        for r in range(0, B, 32):
            level = (raw[shift, r : r + 32, :] - MIDDLE) * STEPS
            level = jnp.clip(level, -32767.0, 32767.0)
            packed[shift, r : r + 32, :] = jnp.round(level).astype(I32).astype(I16)
        departures.append(pltpu.make_async_copy(packed.at[shift], q, out_sems.at[shift]))
        departures[-1].start()
    for copy in departures:
        copy.wait()


def pack(slowness, zones_x, zones_y):
    smem = pl.BlockSpec(memory_space=pltpu.SMEM)
    hbm = pl.BlockSpec(memory_space=pl.ANY)
    return pl.pallas_call(
        pack_kernel,
        out_shape=[jax.ShapeDtypeStruct((B + EXTRA, H), I16)] * 4,
        in_specs=[hbm, smem, smem],
        out_specs=[hbm] * 4,
        scratch_shapes=[
            pltpu.VMEM((SECTIONS, B, H), F32),
            pltpu.VMEM((SECTIONS, B + EXTRA, H), I16),
            pltpu.SemaphoreType.DMA((SECTIONS,)),
            pltpu.SemaphoreType.DMA((SECTIONS,)),
        ],
        name="pack",
    )(slowness, zones_x, zones_y)


def fields_kernel(
    receiver, amp_hbm, source_x_hbm, source_y_hbm, _, rec_mine, rec_send, sources,
    rec, amp, source_x, source_y, spread, fields, in_sems, out_sems,
):
    section, pair, core = place()
    rows = pl.ds(pl.multiple_of(section * B, B), B)
    parts = [
        receiver.at[pl.ds(lax.rem(core + 1 - k, 2) * MINE, MINE), :, rows, :] for k in range(2)
    ]
    arrivals = [
        pltpu.make_async_copy(*ends, in_sems.at[k])
        for k, ends in enumerate(
            (
                (amp_hbm, amp),
                (source_x_hbm, source_x),
                (source_y_hbm, source_y),
                (parts[0], rec.at[0]),
                (parts[1], rec.at[1]),
            )
        )
    ]
    for copy in arrivals:
        copy.start()
    departures = [
        pltpu.make_async_copy(*ends, out_sems.at[k])
        for k, ends in enumerate(((rec.at[0], rec_send), (rec.at[1], rec_mine), (fields, sources)))
    ]
    for copy in arrivals:
        copy.wait()
    for copy in departures[:2]:
        copy.start()
    count = source_x.shape[1]
    cells = lax.broadcasted_iota(I32, (B, count), 0)
    hot_x = jnp.where(cells + section * B == source_x[...], 1.0, 0.0).astype(BF16)
    hot_y = cells + pair * B == source_y[...]
    for f in range(MINE):
        for part in range(2):
            row = amp[pl.ds(core * MINE + f, 1), part, :].astype(F32)
            spread[part * B : (part + 1) * B, :] = jnp.where(hot_y, row, 0.0).astype(BF16)
        fields[f] = lax.dot_general(
            hot_x, spread[...], (((1,), (1,)), ((), ())), preferred_element_type=F32
        ).astype(BF16)
    departures[2].start()
    for copy in departures:
        copy.wait()


def starting_fields(receiver, amp, source_x, source_y, after):
    part = jax.ShapeDtypeStruct((MINE, 2, B, H), BF16)
    field = jax.ShapeDtypeStruct((MINE, B, 2 * B), BF16)
    hbm = pl.BlockSpec(memory_space=pl.ANY)
    return pl.pallas_call(
        fields_kernel,
        out_shape=[part, part, field],
        in_specs=[hbm] * 5,
        out_specs=[hbm] * 3,
        scratch_shapes=[
            pltpu.VMEM((2, MINE, 2, B, H), BF16),
            pltpu.VMEM(amp.shape, BF16),
            pltpu.VMEM(source_x.shape, I32),
            pltpu.VMEM(source_y.shape, I32),
            pltpu.VMEM((2 * B, source_x.shape[1]), BF16),
            pltpu.VMEM((MINE, B, 2 * B), BF16),
            pltpu.SemaphoreType.DMA((5,)),
            pltpu.SemaphoreType.DMA((3,)),
        ],
        cost_estimate=pl.CostEstimate(flops=8 * B**3, bytes_accessed=3 * MB, transcendentals=0),
        name="starting_fields",
    )(receiver, amp, source_x, source_y, after)


def prepare_kernel(inverses, operators, table, sems):
    core = place()[2]
    copies = [
        pltpu.make_async_copy(inverses.at[core * MINE + f], table.at[f], sems.at[f])
        for f in range(MINE)
    ]
    for copy in copies:
        copy.start()
    for f in range(MINE):
        copies[f].wait()
        for zone in range(table.shape[1]):
            real = table[f, zone, 0]
            imag = table[f, zone, 1]
            operators[f, zone, :B, :B] = real
            operators[f, zone, B:, B:] = real
            operators[f, zone, B:, :B] = imag
            operators[f, zone, :B, B:] = -imag


def prepare(inverses):
    zones = inverses.shape[1]
    return pl.pallas_call(
        prepare_kernel,
        out_shape=jax.ShapeDtypeStruct((MINE, zones, 2 * B, 2 * B), BF16),
        in_specs=[pl.BlockSpec(memory_space=pltpu.HBM)],
        out_specs=pl.BlockSpec(memory_space=pltpu.VMEM),
        scratch_shapes=[
            pltpu.VMEM((MINE, zones, 2, B, B), BF16),
            pltpu.SemaphoreType.DMA((MINE,)),
        ],
        compiler_params=pltpu.CompilerParams(vmem_limit_bytes=48 * MB),
        cost_estimate=pl.CostEstimate(flops=0, bytes_accessed=6 * MB, transcendentals=0),
        name="prepare",
    )(inverses)


def continue_kernel(
    omegas, sources, operators, rec_mine, rec_other,
    q0, q1, q2, q3, p0, p1, p2, p3,
    grad_mine, grad_other,
    slow, zones, total, *waves,
):
    section, _, core = place()
    W, X, X32, Y, Y32 = (waves[k : k + MINE] for k in range(0, 5 * MINE, MINE))
    mine = pl.ds(pl.multiple_of(core * H, H), H)
    other = pl.ds(pl.multiple_of((1 - core) * H, H), H)

    for shift, (q, p) in enumerate(((q0, p0), (q1, p1), (q2, p2), (q3, p3))):
        level = lax.bitwise_xor(section, shift)
        for r in range(0, B, 32):
            slow[level, r : r + 32, mine] = q[r : r + 32, :].astype(I32).astype(F32)
            slow[level, r : r + 32, other] = p[r : r + 32, :].astype(I32).astype(F32)
        marks = q[B:, :].astype(I32)
        zones[level, 0] = jnp.max(marks[: EXTRA // 2])
        zones[level, 1] = jnp.max(marks[EXTRA // 2 :])

    for f in range(MINE):
        W[f][:B, :] = sources[f].astype(F32)
        for columns, rec in ((mine, rec_mine), (other, rec_other)):
            W[f][B:, columns] = rec[f, 0].astype(F32)
        imag_mine = pl.ds(pl.multiple_of(B + core * H, H), H)
        imag_other = pl.ds(pl.multiple_of(B + (1 - core) * H, H), H)
        for columns, rec in ((imag_mine, rec_mine), (imag_other, rec_other)):
            W[f][B:, columns] = -rec[f, 1].astype(F32)

    CH, PER = 8, 24

    def rotate(level, f):
        omega = omegas[core * MINE + f]
        scale = omega * (0.5 / math.pi / STEPS)
        base = omega * (0.5 / math.pi * MIDDLE) - 0.5
        for r in range(0, B, CH):
            for c in range(0, B, H):
                turn = slow[level, r : r + CH, c : c + H] * scale + base
                square = turn * turn
                half_sin = turn * horner(square, SIN)
                half_cos = horner(square, COS)
                cosine = half_sin * half_sin - 1.0
                sine = -half_sin * half_cos
                for wave in range(0, 2 * B, B):
                    rows = slice(wave + r, wave + r + CH)
                    columns = slice(wave + c, wave + c + H)
                    real = W[f][rows, c : c + H]
                    imag = W[f][rows, B + c : B + c + H]
                    for down, value in (
                        (r, real * cosine - imag * sine),
                        (B + r, real * sine + imag * cosine),
                    ):
                        X32[f][down : down + CH, columns] = value
                        X[f][down : down + CH, columns] = value.astype(BF16)
                yield

    def inline(level, f):
        zone = zones[level, 0]
        for wave in range(0, 2 * B, B):
            update = jnp.dot(
                operators[f, zone], X[f][:, wave : wave + B], preferred_element_type=F32
            )
            yield
            for part in range(0, 2 * B, B):
                value = X32[f][part : part + B, wave : wave + B] + update[part : part + B]
                Y32[f][wave : wave + B, part : part + B] = value
                Y[f][wave : wave + B, part : part + B] = value.astype(BF16)

    def crossline(level, f):
        zone = zones[level, 1]
        omega = omegas[core * MINE + f]
        for part in range(0, 2 * B, B):
            update = lax.dot_general(
                Y[f][...],
                operators[f, zone, part : part + B, :],
                (((1,), (1,)), ((), ())),
                preferred_element_type=F32,
            )
            yield
            for c in range(0, B, H):
                for r in range(0, B, CH):
                    new = []
                    columns = slice(part + c, part + c + H)
                    for wave in range(0, 2 * B, B):
                        rows = slice(wave + r, wave + r + CH)
                        value = Y32[f][rows, columns] + update[rows, c : c + H]
                        W[f][rows, columns] = value
                        new.append(value)
                    if part > 0:
                        term = W[f][r : r + CH, c : c + H] * W[f][B + r : B + r + CH, c : c + H]
                        term = (term - new[0] * new[1]) * (omega * omega)
                        if f > 0:
                            term += total[c // H, level, r : r + CH, :]
                        total[c // H, level, r : r + CH, :] = term

    def side_by_side(products, others):
        for _ in products:
            for _ in range(PER):
                next(others, None)
        for _ in others:
            pass

    def both(level, f):
        yield from inline(level, f)
        yield from crossline(level, f)

    def one_level(level, carry):
        @pl.when(level < LEVELS)
        def _():
            side_by_side(both(level, 0), rotate(level, 1))

        @pl.when(level >= 0)
        def _():
            following = jnp.minimum(level + 1, LEVELS - 1)
            side_by_side(both(level, 1), rotate(following, 0))

        return carry

    for _ in rotate(0, 0):
        pass
    lax.fori_loop(0, LEVELS, one_level, 0)
    grad_mine[...] = total[core]
    grad_other[...] = total[1 - core].astype(BF16)


def continue_all(omegas, sources, operators, rec_mine, rec_other, mine, other):
    vmem = pl.BlockSpec(memory_space=pltpu.VMEM)
    smem = pl.BlockSpec(memory_space=pltpu.SMEM)
    return pl.pallas_call(
        continue_kernel,
        out_shape=[
            jax.ShapeDtypeStruct((LEVELS, B, H), F32),
            jax.ShapeDtypeStruct((LEVELS, B, H), BF16),
        ],
        in_specs=[smem] + [vmem] * 12,
        out_specs=[vmem, vmem],
        scratch_shapes=[
            pltpu.VMEM((LEVELS, B, B), F32),
            pltpu.SMEM((LEVELS, 2), I32),
            pltpu.VMEM((2, LEVELS, B, H), F32),
            *[pltpu.VMEM((2 * B, 2 * B), kind) for kind in (F32, BF16, F32, BF16, F32) for _ in range(MINE)],
        ],
        compiler_params=pltpu.CompilerParams(vmem_limit_bytes=32 * MB),
        cost_estimate=pl.CostEstimate(
            flops=2 * 128 * B**3, bytes_accessed=8 * MB, transcendentals=0
        ),
        name="continue_levels",
    )(omegas, sources, operators, rec_mine, rec_other, *mine, *other)


def merge_kernel(mine, got, own, s1, s2, s3):
    section, _, _ = place()
    for shift, out in enumerate((own, s1, s2, s3)):
        level = lax.bitwise_xor(section, shift)
        out[...] = (mine[level] + got[level].astype(F32)).astype(out.dtype)


def merge(mine, got):
    vmem = pl.BlockSpec(memory_space=pltpu.VMEM)
    return pl.pallas_call(
        merge_kernel,
        out_shape=[jax.ShapeDtypeStruct((B, H), F32)]
        + [jax.ShapeDtypeStruct((B, H), BF16)] * 3,
        in_specs=[vmem, vmem],
        out_specs=[vmem] * 4,
        compiler_params=pltpu.CompilerParams(vmem_limit_bytes=8 * MB),
        name="merge",
    )(mine, got)


def assemble_kernel(own, g1, g2, g3, out):
    section, _, _ = place()
    for shift, block in enumerate((own, g1, g2, g3)):
        origin = lax.bitwise_xor(section, shift)
        out[0, pl.ds(pl.multiple_of(origin * B, B), B), :] = block[...].astype(F32)


def assemble(own, blocks):
    vmem = pl.BlockSpec(memory_space=pltpu.VMEM)
    return pl.pallas_call(
        assemble_kernel,
        out_shape=jax.ShapeDtypeStruct((1, SECTIONS * B, H), F32),
        in_specs=[vmem] * 4,
        out_specs=vmem,
        compiler_params=pltpu.CompilerParams(vmem_limit_bytes=8 * MB),
        name="assemble",
    )(own, *blocks)


def along_depth(block, shift):
    return lax.ppermute(block, "depth", [(i, i ^ shift) for i in range(SECTIONS)])


def other_core(block):
    count = lax.axis_size("xline")
    return lax.ppermute(block, "xline", [(i, i ^ 1) for i in range(count)])


def per_device(
    receiver_data, source_amp, source_x, source_y, omegas, slowness, inverses, zones_x, zones_y
):
    blocks = pack(slowness, zones_x, zones_y)
    moved = [along_depth(blocks[k], k) for k in (1, 2, 3)]
    rec_mine, rec_send, sources = starting_fields(
        receiver_data, source_amp, source_x.reshape(1, -1), source_y.reshape(1, -1), blocks[0]
    )
    own_other = other_core(blocks[0])
    inverses, sources = lax.optimization_barrier((inverses, sources))
    operators, rec_send, *moved = lax.optimization_barrier(
        (prepare(inverses), rec_send, *moved)
    )
    rec_other = other_core(rec_send)
    mine = [blocks[0], *moved]
    other = [own_other] + [other_core(block) for block in moved]
    grad_mine, grad_other = continue_all(
        omegas, sources, operators, rec_mine, rec_other, mine, other
    )
    own, *parts = merge(grad_mine, other_core(grad_other))
    return assemble(own, [along_depth(parts[k - 1], k) for k in (1, 2, 3)])


def solution(mesh):
    in_specs = (
        P(None, None, None, "xline"),
        P(),
        P(),
        P(),
        P(),
        P("depth", None, "xline"),
        P(),
        P("depth", None),
        P("depth", None),
    )
    return jax.shard_map(
        per_device,
        mesh=mesh,
        in_specs=in_specs,
        out_specs=P("depth", None, "xline"),
        check_vma=False,
    )
```

```python
import math

import jax
import jax.numpy as jnp
from jax import lax
from jax.experimental import pallas as pl
from jax.experimental.pallas import tpu as pltpu
from jax.sharding import PartitionSpec as P

F32 = jnp.float32
BF16 = jnp.bfloat16
I32 = jnp.int32
I16 = jnp.int16

SECTIONS = 4
LEVELS = 4
FREQS = 4
MINE = 2
B = 256
H = 128
EXTRA = 16

MIDDLE = 1.1
STEPS = 36000.0

SIN = (4.4428679, -7.30744341, 3.59478797, -0.78437374)
COS = (1.4142135, -6.97885099, 5.73946117, -1.88356295, 0.3106981)

MB = 1 << 20


def horner(u, coefs):
    total = coefs[-1]
    for c in coefs[-2::-1]:
        total = total * u + c
    return total


def place():
    line = lax.axis_index("xline")
    return lax.axis_index("depth"), line // 2, lax.rem(line, 2)


def pack_kernel(slow, zones_x, zones_y, q0, q1, q2, q3, raw, packed, in_sems, out_sems):
    section, pair, _ = place()
    order = ((1, q1), (2, q2), (3, q3), (0, q0))
    arrivals = []
    for shift, _ in order:
        start = pl.ds(pl.multiple_of(lax.rem(section + shift, SECTIONS) * B, B), B)
        arrivals.append(
            pltpu.make_async_copy(slow.at[0, start, :], raw.at[shift], in_sems.at[shift])
        )
        arrivals[-1].start()
    zone_y = zones_y[0, pair]
    upper = lax.broadcasted_iota(I32, (EXTRA, H), 0) < EXTRA // 2
    departures = []
    for (shift, q), arrival in zip(order, arrivals):
        to = lax.rem(section + shift, SECTIONS)
        packed[shift, B:, :] = jnp.where(upper, zones_x[0, to], zone_y).astype(I16)
        arrival.wait()
        for r in range(0, B, 32):
            level = (raw[shift, r : r + 32, :] - MIDDLE) * STEPS
            level = jnp.clip(level, -32767.0, 32767.0)
            packed[shift, r : r + 32, :] = jnp.round(level).astype(I32).astype(I16)
        departures.append(pltpu.make_async_copy(packed.at[shift], q, out_sems.at[shift]))
        departures[-1].start()
    for copy in departures:
        copy.wait()


def pack(slowness, zones_x, zones_y):
    smem = pl.BlockSpec(memory_space=pltpu.SMEM)
    hbm = pl.BlockSpec(memory_space=pl.ANY)
    return pl.pallas_call(
        pack_kernel,
        out_shape=[jax.ShapeDtypeStruct((B + EXTRA, H), I16)] * 4,
        in_specs=[hbm, smem, smem],
        out_specs=[hbm] * 4,
        scratch_shapes=[
            pltpu.VMEM((SECTIONS, B, H), F32),
            pltpu.VMEM((SECTIONS, B + EXTRA, H), I16),
            pltpu.SemaphoreType.DMA((SECTIONS,)),
            pltpu.SemaphoreType.DMA((SECTIONS,)),
        ],
        name="pack",
    )(slowness, zones_x, zones_y)


def fields_kernel(
    receiver, amp_hbm, source_x_hbm, source_y_hbm, _, rec_mine, rec_send, sources,
    rec, amp, source_x, source_y, spread, fields, in_sems, out_sems,
):
    section, pair, core = place()
    rows = pl.ds(pl.multiple_of(section * B, B), B)
    parts = [
        receiver.at[pl.ds(lax.rem(core + 1 - k, 2) * MINE, MINE), :, rows, :] for k in range(2)
    ]
    arrivals = [
        pltpu.make_async_copy(*ends, in_sems.at[k])
        for k, ends in enumerate(
            (
                (amp_hbm, amp),
                (source_x_hbm, source_x),
                (source_y_hbm, source_y),
                (parts[0], rec.at[0]),
                (parts[1], rec.at[1]),
            )
        )
    ]
    for copy in arrivals:
        copy.start()
    departures = [
        pltpu.make_async_copy(*ends, out_sems.at[k])
        for k, ends in enumerate(((rec.at[0], rec_send), (rec.at[1], rec_mine), (fields, sources)))
    ]
    for copy in arrivals:
        copy.wait()
    for copy in departures[:2]:
        copy.start()
    count = source_x.shape[1]
    cells = lax.broadcasted_iota(I32, (B, count), 0)
    hot_x = jnp.where(cells + section * B == source_x[...], 1.0, 0.0).astype(BF16)
    hot_y = cells + pair * B == source_y[...]
    for f in range(MINE):
        for part in range(2):
            row = amp[pl.ds(core * MINE + f, 1), part, :].astype(F32)
            spread[part * B : (part + 1) * B, :] = jnp.where(hot_y, row, 0.0).astype(BF16)
        fields[f] = lax.dot_general(
            hot_x, spread[...], (((1,), (1,)), ((), ())), preferred_element_type=F32
        ).astype(BF16)
    departures[2].start()
    for copy in departures:
        copy.wait()


def starting_fields(receiver, amp, source_x, source_y, after):
    part = jax.ShapeDtypeStruct((MINE, 2, B, H), BF16)
    field = jax.ShapeDtypeStruct((MINE, B, 2 * B), BF16)
    hbm = pl.BlockSpec(memory_space=pl.ANY)
    return pl.pallas_call(
        fields_kernel,
        out_shape=[part, part, field],
        in_specs=[hbm] * 5,
        out_specs=[hbm] * 3,
        scratch_shapes=[
            pltpu.VMEM((2, MINE, 2, B, H), BF16),
            pltpu.VMEM(amp.shape, BF16),
            pltpu.VMEM(source_x.shape, I32),
            pltpu.VMEM(source_y.shape, I32),
            pltpu.VMEM((2 * B, source_x.shape[1]), BF16),
            pltpu.VMEM((MINE, B, 2 * B), BF16),
            pltpu.SemaphoreType.DMA((5,)),
            pltpu.SemaphoreType.DMA((3,)),
        ],
        cost_estimate=pl.CostEstimate(flops=8 * B**3, bytes_accessed=3 * MB, transcendentals=0),
        name="starting_fields",
    )(receiver, amp, source_x, source_y, after)


def prepare_kernel(inverses, operators, table, sems):
    core = place()[2]
    copies = [
        pltpu.make_async_copy(inverses.at[core * MINE + f], table.at[f], sems.at[f])
        for f in range(MINE)
    ]
    for copy in copies:
        copy.start()
    for f in range(MINE):
        copies[f].wait()
        for zone in range(table.shape[1]):
            real = table[f, zone, 0]
            imag = table[f, zone, 1]
            operators[f, zone, :B, :B] = real
            operators[f, zone, B:, B:] = real
            operators[f, zone, B:, :B] = imag
            operators[f, zone, :B, B:] = -imag


def prepare(inverses):
    zones = inverses.shape[1]
    return pl.pallas_call(
        prepare_kernel,
        out_shape=jax.ShapeDtypeStruct((MINE, zones, 2 * B, 2 * B), BF16),
        in_specs=[pl.BlockSpec(memory_space=pltpu.HBM)],
        out_specs=pl.BlockSpec(memory_space=pltpu.VMEM),
        scratch_shapes=[
            pltpu.VMEM((MINE, zones, 2, B, B), BF16),
            pltpu.SemaphoreType.DMA((MINE,)),
        ],
        compiler_params=pltpu.CompilerParams(vmem_limit_bytes=48 * MB),
        cost_estimate=pl.CostEstimate(flops=0, bytes_accessed=6 * MB, transcendentals=0),
        name="prepare",
    )(inverses)


def continue_kernel(
    omegas, sources, operators, rec_mine, rec_other,
    q0, q1, q2, q3, p0, p1, p2, p3,
    grad_mine, grad_other,
    slow, zones, total, *waves,
):
    section, _, core = place()
    W, X, X32, Y, Y32 = (waves[k : k + MINE] for k in range(0, 5 * MINE, MINE))
    mine = pl.ds(pl.multiple_of(core * H, H), H)
    other = pl.ds(pl.multiple_of((1 - core) * H, H), H)

    for shift, (q, p) in enumerate(((q0, p0), (q1, p1), (q2, p2), (q3, p3))):
        level = lax.rem(section + SECTIONS - shift, SECTIONS)
        for r in range(0, B, 32):
            slow[level, r : r + 32, mine] = q[r : r + 32, :].astype(I32).astype(F32)
            slow[level, r : r + 32, other] = p[r : r + 32, :].astype(I32).astype(F32)
        marks = q[B:, :].astype(I32)
        zones[level, 0] = jnp.max(marks[: EXTRA // 2])
        zones[level, 1] = jnp.max(marks[EXTRA // 2 :])

    for f in range(MINE):
        W[f][:B, :] = sources[f].astype(F32)
        for columns, rec in ((mine, rec_mine), (other, rec_other)):
            W[f][B:, columns] = rec[f, 0].astype(F32)
        imag_mine = pl.ds(pl.multiple_of(B + core * H, H), H)
        imag_other = pl.ds(pl.multiple_of(B + (1 - core) * H, H), H)
        for columns, rec in ((imag_mine, rec_mine), (imag_other, rec_other)):
            W[f][B:, columns] = -rec[f, 1].astype(F32)

    CH, PER = 8, 24

    def rotate(level, f):
        omega = omegas[core * MINE + f]
        scale = omega * (0.5 / math.pi / STEPS)
        base = omega * (0.5 / math.pi * MIDDLE) - 0.5
        for r in range(0, B, CH):
            for c in range(0, B, H):
                turn = slow[level, r : r + CH, c : c + H] * scale + base
                square = turn * turn
                half_sin = turn * horner(square, SIN)
                half_cos = horner(square, COS)
                cosine = half_sin * half_sin - 1.0
                sine = -half_sin * half_cos
                for wave in range(0, 2 * B, B):
                    rows = slice(wave + r, wave + r + CH)
                    columns = slice(wave + c, wave + c + H)
                    real = W[f][rows, c : c + H]
                    imag = W[f][rows, B + c : B + c + H]
                    for down, value in (
                        (r, real * cosine - imag * sine),
                        (B + r, real * sine + imag * cosine),
                    ):
                        X32[f][down : down + CH, columns] = value
                        X[f][down : down + CH, columns] = value.astype(BF16)
                yield

    def inline(level, f):
        zone = zones[level, 0]
        for wave in range(0, 2 * B, B):
            update = jnp.dot(
                operators[f, zone], X[f][:, wave : wave + B], preferred_element_type=F32
            )
            yield
            for part in range(0, 2 * B, B):
                value = X32[f][part : part + B, wave : wave + B] + update[part : part + B]
                Y32[f][wave : wave + B, part : part + B] = value
                Y[f][wave : wave + B, part : part + B] = value.astype(BF16)

    def crossline(level, f):
        zone = zones[level, 1]
        omega = omegas[core * MINE + f]
        for part in range(0, 2 * B, B):
            update = lax.dot_general(
                Y[f][...],
                operators[f, zone, part : part + B, :],
                (((1,), (1,)), ((), ())),
                preferred_element_type=F32,
            )
            yield
            for c in range(0, B, H):
                for r in range(0, B, CH):
                    new = []
                    columns = slice(part + c, part + c + H)
                    for wave in range(0, 2 * B, B):
                        rows = slice(wave + r, wave + r + CH)
                        value = Y32[f][rows, columns] + update[rows, c : c + H]
                        W[f][rows, columns] = value
                        new.append(value)
                    if part > 0:
                        term = W[f][r : r + CH, c : c + H] * W[f][B + r : B + r + CH, c : c + H]
                        term = (term - new[0] * new[1]) * (omega * omega)
                        if f > 0:
                            term += total[c // H, level, r : r + CH, :]
                        total[c // H, level, r : r + CH, :] = term

    def side_by_side(products, others):
        for _ in products:
            for _ in range(PER):
                next(others, None)
        for _ in others:
            pass

    def both(level, f):
        yield from inline(level, f)
        yield from crossline(level, f)

    def one_level(level, carry):
        @pl.when(level < LEVELS)
        def _():
            side_by_side(both(level, 0), rotate(level, 1))

        @pl.when(level >= 0)
        def _():
            following = jnp.minimum(level + 1, LEVELS - 1)
            side_by_side(both(level, 1), rotate(following, 0))

        return carry

    for _ in rotate(0, 0):
        pass
    lax.fori_loop(0, LEVELS, one_level, 0)
    grad_mine[...] = total[core]
    grad_other[...] = total[1 - core].astype(BF16)


def continue_all(omegas, sources, operators, rec_mine, rec_other, mine, other):
    vmem = pl.BlockSpec(memory_space=pltpu.VMEM)
    smem = pl.BlockSpec(memory_space=pltpu.SMEM)
    return pl.pallas_call(
        continue_kernel,
        out_shape=[
            jax.ShapeDtypeStruct((LEVELS, B, H), F32),
            jax.ShapeDtypeStruct((LEVELS, B, H), BF16),
        ],
        in_specs=[smem] + [vmem] * 12,
        out_specs=[vmem, vmem],
        scratch_shapes=[
            pltpu.VMEM((LEVELS, B, B), F32),
            pltpu.SMEM((LEVELS, 2), I32),
            pltpu.VMEM((2, LEVELS, B, H), F32),
            *[pltpu.VMEM((2 * B, 2 * B), kind) for kind in (F32, BF16, F32, BF16, F32) for _ in range(MINE)],
        ],
        compiler_params=pltpu.CompilerParams(vmem_limit_bytes=32 * MB),
        cost_estimate=pl.CostEstimate(
            flops=2 * 128 * B**3, bytes_accessed=8 * MB, transcendentals=0
        ),
        name="continue_levels",
    )(omegas, sources, operators, rec_mine, rec_other, *mine, *other)


def merge_kernel(mine, got, own, s1, s2, s3):
    section, _, _ = place()
    for shift, out in enumerate((own, s1, s2, s3)):
        level = lax.rem(section + shift, SECTIONS)
        out[...] = (mine[level] + got[level].astype(F32)).astype(out.dtype)


def merge(mine, got):
    vmem = pl.BlockSpec(memory_space=pltpu.VMEM)
    return pl.pallas_call(
        merge_kernel,
        out_shape=[jax.ShapeDtypeStruct((B, H), F32)]
        + [jax.ShapeDtypeStruct((B, H), BF16)] * 3,
        in_specs=[vmem, vmem],
        out_specs=[vmem] * 4,
        compiler_params=pltpu.CompilerParams(vmem_limit_bytes=8 * MB),
        name="merge",
    )(mine, got)


def assemble_kernel(own, g1, g2, g3, out):
    section, _, _ = place()
    for shift, block in enumerate((own, g1, g2, g3)):
        origin = lax.rem(section + SECTIONS - shift, SECTIONS)
        out[0, pl.ds(pl.multiple_of(origin * B, B), B), :] = block[...].astype(F32)


def assemble(own, blocks):
    vmem = pl.BlockSpec(memory_space=pltpu.VMEM)
    return pl.pallas_call(
        assemble_kernel,
        out_shape=jax.ShapeDtypeStruct((1, SECTIONS * B, H), F32),
        in_specs=[vmem] * 4,
        out_specs=vmem,
        compiler_params=pltpu.CompilerParams(vmem_limit_bytes=8 * MB),
        name="assemble",
    )(own, *blocks)


def along_depth(block, shift):
    return lax.ppermute(block, "depth", [(i, (i + shift) % SECTIONS) for i in range(SECTIONS)])


def other_core(block):
    count = lax.axis_size("xline")
    return lax.ppermute(block, "xline", [(i, i ^ 1) for i in range(count)])


def per_device(
    receiver_data, source_amp, source_x, source_y, omegas, slowness, inverses, zones_x, zones_y
):
    blocks = pack(slowness, zones_x, zones_y)
    moved = [along_depth(blocks[k], k) for k in (1, 2, 3)]
    rec_mine, rec_send, sources = starting_fields(
        receiver_data, source_amp, source_x.reshape(1, -1), source_y.reshape(1, -1), blocks[0]
    )
    own_other = other_core(blocks[0])
    inverses, sources = lax.optimization_barrier((inverses, sources))
    operators, rec_send, *moved = lax.optimization_barrier(
        (prepare(inverses), rec_send, *moved)
    )
    rec_other = other_core(rec_send)
    mine = [blocks[0], *moved]
    other = [own_other] + [other_core(block) for block in moved]
    grad_mine, grad_other = continue_all(
        omegas, sources, operators, rec_mine, rec_other, mine, other
    )
    own, *parts = merge(grad_mine, other_core(grad_other))
    return assemble(own, [along_depth(parts[k - 1], k) for k in (1, 2, 3)])


def solution(mesh):
    in_specs = (
        P(None, None, None, "xline"),
        P(),
        P(),
        P(),
        P(),
        P("depth", None, "xline"),
        P(),
        P("depth", None),
        P("depth", None),
    )
    return jax.shard_map(
        per_device,
        mesh=mesh,
        in_specs=in_specs,
        out_specs=P("depth", None, "xline"),
        check_vma=False,
    )
```

```python
import math

import jax
import jax.numpy as jnp
from jax import lax
from jax.experimental import pallas as pl
from jax.experimental.pallas import tpu as pltpu
from jax.sharding import PartitionSpec as P

F32 = jnp.float32
BF16 = jnp.bfloat16
I32 = jnp.int32
I16 = jnp.int16

SECTIONS = 4
LEVELS = 4
FREQS = 4
MINE = 2
B = 256
H = 128
EXTRA = 16

MIDDLE = 1.1
STEPS = 36000.0

SIN = (4.4428679, -7.30744341, 3.59478797, -0.78437374)
COS = (1.4142135, -6.97885099, 5.73946117, -1.88356295, 0.3106981)

MB = 1 << 20


def horner(u, coefs):
    total = coefs[-1]
    for c in coefs[-2::-1]:
        total = total * u + c
    return total


def place():
    line = lax.axis_index("xline")
    return lax.axis_index("depth"), line // 2, lax.rem(line, 2)


def pack_kernel(slow, zones_x, zones_y, q0, q1, q2, q3, raw, packed, in_sems, out_sems):
    section, pair, _ = place()
    order = ((1, q1), (2, q2), (3, q3), (0, q0))
    arrivals = []
    for shift, _ in order:
        start = pl.ds(pl.multiple_of(lax.rem(section + shift, SECTIONS) * B, B), B)
        arrivals.append(
            pltpu.make_async_copy(slow.at[0, start, :], raw.at[shift], in_sems.at[shift])
        )
        arrivals[-1].start()
    zone_y = zones_y[0, pair]
    upper = lax.broadcasted_iota(I32, (EXTRA, H), 0) < EXTRA // 2
    departures = []
    for (shift, q), arrival in zip(order, arrivals):
        to = lax.rem(section + shift, SECTIONS)
        packed[shift, B:, :] = jnp.where(upper, zones_x[0, to], zone_y).astype(I16)
        arrival.wait()
        for r in range(0, B, 32):
            level = (raw[shift, r : r + 32, :] - MIDDLE) * STEPS
            level = jnp.clip(level, -32767.0, 32767.0)
            packed[shift, r : r + 32, :] = jnp.round(level).astype(I32).astype(I16)
        departures.append(pltpu.make_async_copy(packed.at[shift], q, out_sems.at[shift]))
        departures[-1].start()
    for copy in departures:
        copy.wait()


def pack(slowness, zones_x, zones_y):
    smem = pl.BlockSpec(memory_space=pltpu.SMEM)
    hbm = pl.BlockSpec(memory_space=pl.ANY)
    return pl.pallas_call(
        pack_kernel,
        out_shape=[jax.ShapeDtypeStruct((B + EXTRA, H), I16)] * 4,
        in_specs=[hbm, smem, smem],
        out_specs=[hbm] * 4,
        scratch_shapes=[
            pltpu.VMEM((SECTIONS, B, H), F32),
            pltpu.VMEM((SECTIONS, B + EXTRA, H), I16),
            pltpu.SemaphoreType.DMA((SECTIONS,)),
            pltpu.SemaphoreType.DMA((SECTIONS,)),
        ],
        name="pack",
    )(slowness, zones_x, zones_y)


def fields_kernel(
    receiver, amp_hbm, source_x_hbm, source_y_hbm, _, rec_mine, rec_send, sources,
    rec, amp, source_x, source_y, spread, fields, in_sems, out_sems,
):
    section, pair, core = place()
    rows = pl.ds(pl.multiple_of(section * B, B), B)
    parts = [
        receiver.at[pl.ds(lax.rem(core + 1 - k, 2) * MINE, MINE), :, rows, :] for k in range(2)
    ]
    arrivals = [
        pltpu.make_async_copy(*ends, in_sems.at[k])
        for k, ends in enumerate(
            (
                (amp_hbm, amp),
                (source_x_hbm, source_x),
                (source_y_hbm, source_y),
                (parts[0], rec.at[0]),
                (parts[1], rec.at[1]),
            )
        )
    ]
    for copy in arrivals:
        copy.start()
    departures = [
        pltpu.make_async_copy(*ends, out_sems.at[k])
        for k, ends in enumerate(((rec.at[0], rec_send), (rec.at[1], rec_mine), (fields, sources)))
    ]
    for copy in arrivals:
        copy.wait()
    for copy in departures[:2]:
        copy.start()
    count = source_x.shape[1]
    cells = lax.broadcasted_iota(I32, (B, count), 0)
    hot_x = jnp.where(cells + section * B == source_x[...], 1.0, 0.0).astype(BF16)
    hot_y = cells + pair * B == source_y[...]
    for f in range(MINE):
        for part in range(2):
            row = amp[pl.ds(core * MINE + f, 1), part, :].astype(F32)
            spread[part * B : (part + 1) * B, :] = jnp.where(hot_y, row, 0.0).astype(BF16)
        fields[f] = lax.dot_general(
            hot_x, spread[...], (((1,), (1,)), ((), ())), preferred_element_type=F32
        ).astype(BF16)
    departures[2].start()
    for copy in departures:
        copy.wait()


def starting_fields(receiver, amp, source_x, source_y, after):
    part = jax.ShapeDtypeStruct((MINE, 2, B, H), BF16)
    field = jax.ShapeDtypeStruct((MINE, B, 2 * B), BF16)
    hbm = pl.BlockSpec(memory_space=pl.ANY)
    return pl.pallas_call(
        fields_kernel,
        out_shape=[part, part, field],
        in_specs=[hbm] * 5,
        out_specs=[hbm] * 3,
        scratch_shapes=[
            pltpu.VMEM((2, MINE, 2, B, H), BF16),
            pltpu.VMEM(amp.shape, BF16),
            pltpu.VMEM(source_x.shape, I32),
            pltpu.VMEM(source_y.shape, I32),
            pltpu.VMEM((2 * B, source_x.shape[1]), BF16),
            pltpu.VMEM((MINE, B, 2 * B), BF16),
            pltpu.SemaphoreType.DMA((5,)),
            pltpu.SemaphoreType.DMA((3,)),
        ],
        cost_estimate=pl.CostEstimate(flops=8 * B**3, bytes_accessed=3 * MB, transcendentals=0),
        name="starting_fields",
    )(receiver, amp, source_x, source_y, after)


def prepare_kernel(inverses, operators, table, sems):
    core = place()[2]
    copies = [
        pltpu.make_async_copy(inverses.at[core * MINE + f], table.at[f], sems.at[f])
        for f in range(MINE)
    ]
    for copy in copies:
        copy.start()
    for f in range(MINE):
        copies[f].wait()
        for zone in range(table.shape[1]):
            real = table[f, zone, 0]
            imag = table[f, zone, 1]
            operators[f, zone, :B, :B] = real
            operators[f, zone, B:, B:] = real
            operators[f, zone, B:, :B] = imag
            operators[f, zone, :B, B:] = -imag


def prepare(inverses):
    zones = inverses.shape[1]
    return pl.pallas_call(
        prepare_kernel,
        out_shape=jax.ShapeDtypeStruct((MINE, zones, 2 * B, 2 * B), BF16),
        in_specs=[pl.BlockSpec(memory_space=pltpu.HBM)],
        out_specs=pl.BlockSpec(memory_space=pltpu.VMEM),
        scratch_shapes=[
            pltpu.VMEM((MINE, zones, 2, B, B), BF16),
            pltpu.SemaphoreType.DMA((MINE,)),
        ],
        compiler_params=pltpu.CompilerParams(vmem_limit_bytes=48 * MB),
        cost_estimate=pl.CostEstimate(flops=0, bytes_accessed=6 * MB, transcendentals=0),
        name="prepare",
    )(inverses)


def continue_kernel(
    omegas, sources, operators, rec_mine, rec_other,
    q0, q1, q2, q3, p0, p1, p2, p3,
    grad_mine, grad_other,
    slow, zones, total, *waves,
):
    section, _, core = place()
    W, X, X32, Y, Y32 = (waves[k : k + MINE] for k in range(0, 5 * MINE, MINE))
    mine = pl.ds(pl.multiple_of(core * H, H), H)
    other = pl.ds(pl.multiple_of((1 - core) * H, H), H)

    for shift, (q, p) in enumerate(((q0, p0), (q1, p1), (q2, p2), (q3, p3))):
        level = lax.rem(section + SECTIONS - shift, SECTIONS)
        for r in range(0, B, 32):
            slow[level, r : r + 32, mine] = q[r : r + 32, :].astype(I32).astype(F32)
            slow[level, r : r + 32, other] = p[r : r + 32, :].astype(I32).astype(F32)
        marks = q[B:, :].astype(I32)
        zones[level, 0] = jnp.max(marks[: EXTRA // 2])
        zones[level, 1] = jnp.max(marks[EXTRA // 2 :])

    for f in range(MINE):
        W[f][:B, :] = sources[f].astype(F32)
        for columns, rec in ((mine, rec_mine), (other, rec_other)):
            W[f][B:, columns] = rec[f, 0].astype(F32)
        imag_mine = pl.ds(pl.multiple_of(B + core * H, H), H)
        imag_other = pl.ds(pl.multiple_of(B + (1 - core) * H, H), H)
        for columns, rec in ((imag_mine, rec_mine), (imag_other, rec_other)):
            W[f][B:, columns] = -rec[f, 1].astype(F32)

    CH, PER = 8, 24

    def rotate(level, f):
        omega = omegas[core * MINE + f]
        scale = omega * (0.5 / math.pi / STEPS)
        base = omega * (0.5 / math.pi * MIDDLE) - 0.5
        for r in range(0, B, CH):
            for c in range(0, B, H):
                turn = slow[level, r : r + CH, c : c + H] * scale + base
                square = turn * turn
                half_sin = turn * horner(square, SIN)
                half_cos = horner(square, COS)
                cosine = half_sin * half_sin - 1.0
                sine = -half_sin * half_cos
                for wave in range(0, 2 * B, B):
                    rows = slice(wave + r, wave + r + CH)
                    columns = slice(wave + c, wave + c + H)
                    real = W[f][rows, c : c + H]
                    imag = W[f][rows, B + c : B + c + H]
                    for down, value in (
                        (r, real * cosine - imag * sine),
                        (B + r, real * sine + imag * cosine),
                    ):
                        X32[f][down : down + CH, columns] = value
                        X[f][down : down + CH, columns] = value.astype(BF16)
                yield

    def inline(level, f):
        zone = zones[level, 0]
        for wave in range(0, 2 * B, B):
            update = jnp.dot(
                operators[f, zone], X[f][:, wave : wave + B], preferred_element_type=F32
            )
            yield
            for part in range(0, 2 * B, B):
                value = X32[f][part : part + B, wave : wave + B] + update[part : part + B]
                Y32[f][wave : wave + B, part : part + B] = value
                Y[f][wave : wave + B, part : part + B] = value.astype(BF16)

    def crossline(level, f):
        zone = zones[level, 1]
        omega = omegas[core * MINE + f]
        for part in range(0, 2 * B, B):
            update = lax.dot_general(
                Y[f][...],
                operators[f, zone, part : part + B, :],
                (((1,), (1,)), ((), ())),
                preferred_element_type=F32,
            )
            yield
            for c in range(0, B, H):
                for r in range(0, B, CH):
                    new = []
                    columns = slice(part + c, part + c + H)
                    for wave in range(0, 2 * B, B):
                        rows = slice(wave + r, wave + r + CH)
                        value = Y32[f][rows, columns] + update[rows, c : c + H]
                        W[f][rows, columns] = value
                        new.append(value)
                    if part > 0:
                        term = W[f][r : r + CH, c : c + H] * W[f][B + r : B + r + CH, c : c + H]
                        term = (term - new[0] * new[1]) * (omega * omega)
                        if f > 0:
                            term += total[c // H, level, r : r + CH, :]
                        total[c // H, level, r : r + CH, :] = term

    def side_by_side(products, others):
        for _ in products:
            for _ in range(PER):
                next(others, None)
        for _ in others:
            pass

    def both(level, f):
        yield from inline(level, f)
        yield from crossline(level, f)

    def one_level(level, carry):
        @pl.when(level < LEVELS)
        def _():
            side_by_side(both(level, 0), rotate(level, 1))

        @pl.when(level >= 0)
        def _():
            following = jnp.minimum(level + 1, LEVELS - 1)
            side_by_side(both(level, 1), rotate(following, 0))

        return carry

    for _ in rotate(0, 0):
        pass
    lax.fori_loop(0, LEVELS, one_level, 0)
    grad_mine[...] = total[core]
    grad_other[...] = total[1 - core].astype(BF16)


def continue_all(omegas, sources, operators, rec_mine, rec_other, mine, other):
    vmem = pl.BlockSpec(memory_space=pltpu.VMEM)
    smem = pl.BlockSpec(memory_space=pltpu.SMEM)
    return pl.pallas_call(
        continue_kernel,
        out_shape=[
            jax.ShapeDtypeStruct((LEVELS, B, H), F32),
            jax.ShapeDtypeStruct((LEVELS, B, H), BF16),
        ],
        in_specs=[smem] + [vmem] * 12,
        out_specs=[vmem, vmem],
        scratch_shapes=[
            pltpu.VMEM((LEVELS, B, B), F32),
            pltpu.SMEM((LEVELS, 2), I32),
            pltpu.VMEM((2, LEVELS, B, H), F32),
            *[pltpu.VMEM((2 * B, 2 * B), kind) for kind in (F32, BF16, F32, BF16, F32) for _ in range(MINE)],
        ],
        compiler_params=pltpu.CompilerParams(vmem_limit_bytes=32 * MB),
        cost_estimate=pl.CostEstimate(
            flops=2 * 128 * B**3, bytes_accessed=8 * MB, transcendentals=0
        ),
        name="continue_levels",
    )(omegas, sources, operators, rec_mine, rec_other, *mine, *other)


def merge_kernel(mine, got, own, s1, s2, s3):
    section, _, _ = place()
    for shift, out in enumerate((own, s1, s2, s3)):
        level = lax.rem(section + shift, SECTIONS)
        out[...] = (mine[level] + got[level].astype(F32)).astype(out.dtype)


def merge(mine, got):
    vmem = pl.BlockSpec(memory_space=pltpu.VMEM)
    return pl.pallas_call(
        merge_kernel,
        out_shape=[jax.ShapeDtypeStruct((B, H), F32)]
        + [jax.ShapeDtypeStruct((B, H), BF16)] * 3,
        in_specs=[vmem, vmem],
        out_specs=[vmem] * 4,
        compiler_params=pltpu.CompilerParams(vmem_limit_bytes=8 * MB),
        name="merge",
    )(mine, got)


def assemble_kernel(own, g1, g2, g3, out):
    section, _, _ = place()
    for shift, block in enumerate((own, g1, g2, g3)):
        origin = lax.rem(section + SECTIONS - shift, SECTIONS)
        out[0, pl.ds(pl.multiple_of(origin * B, B), B), :] = block[...].astype(F32)


def assemble(own, blocks):
    vmem = pl.BlockSpec(memory_space=pltpu.VMEM)
    return pl.pallas_call(
        assemble_kernel,
        out_shape=jax.ShapeDtypeStruct((1, SECTIONS * B, H), F32),
        in_specs=[vmem] * 4,
        out_specs=vmem,
        compiler_params=pltpu.CompilerParams(vmem_limit_bytes=8 * MB),
        name="assemble",
    )(own, *blocks)


def along_depth(block, shift):
    return lax.ppermute(block, "depth", [(i, (i + shift) % SECTIONS) for i in range(SECTIONS)])


def other_core(block):
    count = lax.axis_size("xline")
    return lax.ppermute(block, "xline", [(i, i ^ 1) for i in range(count)])


def per_device(
    receiver_data, source_amp, source_x, source_y, omegas, slowness, inverses, zones_x, zones_y
):
    blocks = pack(slowness, zones_x, zones_y)
    moved = [along_depth(blocks[k], k) for k in (1, 2, 3)]
    rec_mine, rec_send, sources = starting_fields(
        receiver_data, source_amp, source_x.reshape(1, -1), source_y.reshape(1, -1), blocks[0]
    )
    own_other = other_core(blocks[0])
    inverses, rec_send, *moved = lax.optimization_barrier((inverses, rec_send, *moved))
    rec_other = other_core(rec_send)
    operators = prepare(inverses)
    mine = [blocks[0], *moved]
    other = [own_other] + [other_core(block) for block in moved]
    grad_mine, grad_other = continue_all(
        omegas, sources, operators, rec_mine, rec_other, mine, other
    )
    own, *parts = merge(grad_mine, other_core(grad_other))
    return assemble(own, [along_depth(parts[k - 1], k) for k in (1, 2, 3)])


def solution(mesh):
    in_specs = (
        P(None, None, None, "xline"),
        P(),
        P(),
        P(),
        P(),
        P("depth", None, "xline"),
        P(),
        P("depth", None),
        P("depth", None),
    )
    return jax.shard_map(
        per_device,
        mesh=mesh,
        in_specs=in_specs,
        out_specs=P("depth", None, "xline"),
        check_vma=False,
    )
```

```python
import math

import jax
import jax.numpy as jnp
from jax import lax
from jax.experimental import pallas as pl
from jax.experimental.pallas import tpu as pltpu
from jax.sharding import PartitionSpec as P

F32 = jnp.float32
BF16 = jnp.bfloat16
I32 = jnp.int32
I16 = jnp.int16

SECTIONS = 4
LEVELS = 4
FREQS = 4
MINE = 2
B = 256
H = 128
ORDER = (0, 2, 1, 3)
EXTRA = 16

MIDDLE = 1.1
STEPS = 36000.0

SIN = (4.4428679, -7.30744341, 3.59478797, -0.78437374)
COS = (1.4142135, -6.97885099, 5.73946117, -1.88356295, 0.3106981)

MB = 1 << 20


def horner(u, coefs):
    total = coefs[-1]
    for c in coefs[-2::-1]:
        total = total * u + c
    return total


def place():
    line = lax.axis_index("xline")
    return lax.axis_index("depth"), line // 2, lax.rem(line, 2)


def pack_kernel(slow, zones_x, zones_y, q0, q1, q2, q3, raw, packed, in_sems, out_sems):
    section, pair, _ = place()
    order = tuple(zip(ORDER, (q0, q1, q2, q3)))
    order = order[1:] + order[:1]
    arrivals = []
    for shift, _ in order:
        start = pl.ds(pl.multiple_of(lax.rem(section + shift, SECTIONS) * B, B), B)
        arrivals.append(
            pltpu.make_async_copy(slow.at[0, start, :], raw.at[shift], in_sems.at[shift])
        )
        arrivals[-1].start()
    zone_y = zones_y[0, pair]
    upper = lax.broadcasted_iota(I32, (EXTRA, H), 0) < EXTRA // 2
    departures = []
    for (shift, q), arrival in zip(order, arrivals):
        to = lax.rem(section + shift, SECTIONS)
        packed[shift, B:, :] = jnp.where(upper, zones_x[0, to], zone_y).astype(I16)
        arrival.wait()
        for r in range(0, B, 32):
            level = (raw[shift, r : r + 32, :] - MIDDLE) * STEPS
            level = jnp.clip(level, -32767.0, 32767.0)
            packed[shift, r : r + 32, :] = jnp.round(level).astype(I32).astype(I16)
        departures.append(pltpu.make_async_copy(packed.at[shift], q, out_sems.at[shift]))
        departures[-1].start()
    for copy in departures:
        copy.wait()


def pack(slowness, zones_x, zones_y):
    smem = pl.BlockSpec(memory_space=pltpu.SMEM)
    hbm = pl.BlockSpec(memory_space=pl.ANY)
    return pl.pallas_call(
        pack_kernel,
        out_shape=[jax.ShapeDtypeStruct((B + EXTRA, H), I16)] * 4,
        in_specs=[hbm, smem, smem],
        out_specs=[hbm] * 4,
        scratch_shapes=[
            pltpu.VMEM((SECTIONS, B, H), F32),
            pltpu.VMEM((SECTIONS, B + EXTRA, H), I16),
            pltpu.SemaphoreType.DMA((SECTIONS,)),
            pltpu.SemaphoreType.DMA((SECTIONS,)),
        ],
        name="pack",
    )(slowness, zones_x, zones_y)


def fields_kernel(
    receiver, amp_hbm, source_x_hbm, source_y_hbm, _, rec_mine, rec_send, sources,
    rec, amp, source_x, source_y, spread, fields, in_sems, out_sems,
):
    section, pair, core = place()
    rows = pl.ds(pl.multiple_of(section * B, B), B)
    parts = [
        receiver.at[pl.ds(lax.rem(core + 1 - k, 2) * MINE, MINE), :, rows, :] for k in range(2)
    ]
    arrivals = [
        pltpu.make_async_copy(*ends, in_sems.at[k])
        for k, ends in enumerate(
            (
                (amp_hbm, amp),
                (source_x_hbm, source_x),
                (source_y_hbm, source_y),
                (parts[0], rec.at[0]),
                (parts[1], rec.at[1]),
            )
        )
    ]
    for copy in arrivals:
        copy.start()
    departures = [
        pltpu.make_async_copy(*ends, out_sems.at[k])
        for k, ends in enumerate(((rec.at[0], rec_send), (rec.at[1], rec_mine), (fields, sources)))
    ]
    for copy in arrivals:
        copy.wait()
    for copy in departures[:2]:
        copy.start()
    count = source_x.shape[1]
    cells = lax.broadcasted_iota(I32, (B, count), 0)
    hot_x = jnp.where(cells + section * B == source_x[...], 1.0, 0.0).astype(BF16)
    hot_y = cells + pair * B == source_y[...]
    for f in range(MINE):
        for part in range(2):
            row = amp[pl.ds(core * MINE + f, 1), part, :].astype(F32)
            spread[part * B : (part + 1) * B, :] = jnp.where(hot_y, row, 0.0).astype(BF16)
        fields[f] = lax.dot_general(
            hot_x, spread[...], (((1,), (1,)), ((), ())), preferred_element_type=F32
        ).astype(BF16)
    departures[2].start()
    for copy in departures:
        copy.wait()


def starting_fields(receiver, amp, source_x, source_y, after):
    part = jax.ShapeDtypeStruct((MINE, 2, B, H), BF16)
    field = jax.ShapeDtypeStruct((MINE, B, 2 * B), BF16)
    hbm = pl.BlockSpec(memory_space=pl.ANY)
    return pl.pallas_call(
        fields_kernel,
        out_shape=[part, part, field],
        in_specs=[hbm] * 5,
        out_specs=[hbm] * 3,
        scratch_shapes=[
            pltpu.VMEM((2, MINE, 2, B, H), BF16),
            pltpu.VMEM(amp.shape, BF16),
            pltpu.VMEM(source_x.shape, I32),
            pltpu.VMEM(source_y.shape, I32),
            pltpu.VMEM((2 * B, source_x.shape[1]), BF16),
            pltpu.VMEM((MINE, B, 2 * B), BF16),
            pltpu.SemaphoreType.DMA((5,)),
            pltpu.SemaphoreType.DMA((3,)),
        ],
        cost_estimate=pl.CostEstimate(flops=8 * B**3, bytes_accessed=3 * MB, transcendentals=0),
        name="starting_fields",
    )(receiver, amp, source_x, source_y, after)


def prepare_kernel(inverses, operators, table, sems):
    core = place()[2]
    copies = [
        pltpu.make_async_copy(inverses.at[core * MINE + f], table.at[f], sems.at[f])
        for f in range(MINE)
    ]
    for copy in copies:
        copy.start()
    for f in range(MINE):
        copies[f].wait()
        for zone in range(table.shape[1]):
            real = table[f, zone, 0]
            imag = table[f, zone, 1]
            operators[f, zone, :B, :B] = real
            operators[f, zone, B:, B:] = real
            operators[f, zone, B:, :B] = imag
            operators[f, zone, :B, B:] = -imag


def prepare(inverses):
    zones = inverses.shape[1]
    return pl.pallas_call(
        prepare_kernel,
        out_shape=jax.ShapeDtypeStruct((MINE, zones, 2 * B, 2 * B), BF16),
        in_specs=[pl.BlockSpec(memory_space=pltpu.HBM)],
        out_specs=pl.BlockSpec(memory_space=pltpu.VMEM),
        scratch_shapes=[
            pltpu.VMEM((MINE, zones, 2, B, B), BF16),
            pltpu.SemaphoreType.DMA((MINE,)),
        ],
        compiler_params=pltpu.CompilerParams(vmem_limit_bytes=48 * MB),
        cost_estimate=pl.CostEstimate(flops=0, bytes_accessed=6 * MB, transcendentals=0),
        name="prepare",
    )(inverses)


def continue_kernel(
    omegas, sources, operators, rec_mine, rec_other,
    q0, q1, q2, q3, p0, p1, p2, p3,
    grad_mine, grad_other,
    slow, zones, total, *waves,
):
    section, _, core = place()
    W, X, X32, Y, Y32 = (waves[k : k + MINE] for k in range(0, 5 * MINE, MINE))
    mine = pl.ds(pl.multiple_of(core * H, H), H)
    other = pl.ds(pl.multiple_of((1 - core) * H, H), H)

    for shift, q, p in zip(ORDER, (q0, q1, q2, q3), (p0, p1, p2, p3)):
        level = lax.rem(section + SECTIONS - shift, SECTIONS)
        for r in range(0, B, 32):
            slow[level, r : r + 32, mine] = q[r : r + 32, :].astype(I32).astype(F32)
            slow[level, r : r + 32, other] = p[r : r + 32, :].astype(I32).astype(F32)
        marks = q[B:, :].astype(I32)
        zones[level, 0] = jnp.max(marks[: EXTRA // 2])
        zones[level, 1] = jnp.max(marks[EXTRA // 2 :])

    for f in range(MINE):
        W[f][:B, :] = sources[f].astype(F32)
        for columns, rec in ((mine, rec_mine), (other, rec_other)):
            W[f][B:, columns] = rec[f, 0].astype(F32)
        imag_mine = pl.ds(pl.multiple_of(B + core * H, H), H)
        imag_other = pl.ds(pl.multiple_of(B + (1 - core) * H, H), H)
        for columns, rec in ((imag_mine, rec_mine), (imag_other, rec_other)):
            W[f][B:, columns] = -rec[f, 1].astype(F32)

    CH, PER = 8, 24

    def rotate(level, f):
        omega = omegas[core * MINE + f]
        scale = omega * (0.5 / math.pi / STEPS)
        base = omega * (0.5 / math.pi * MIDDLE) - 0.5
        for r in range(0, B, CH):
            for c in range(0, B, H):
                turn = slow[level, r : r + CH, c : c + H] * scale + base
                square = turn * turn
                half_sin = turn * horner(square, SIN)
                half_cos = horner(square, COS)
                cosine = half_sin * half_sin - 1.0
                sine = -half_sin * half_cos
                for wave in range(0, 2 * B, B):
                    rows = slice(wave + r, wave + r + CH)
                    columns = slice(wave + c, wave + c + H)
                    real = W[f][rows, c : c + H]
                    imag = W[f][rows, B + c : B + c + H]
                    for down, value in (
                        (r, real * cosine - imag * sine),
                        (B + r, real * sine + imag * cosine),
                    ):
                        X32[f][down : down + CH, columns] = value
                        X[f][down : down + CH, columns] = value.astype(BF16)
                yield

    def inline(level, f):
        zone = zones[level, 0]
        for wave in range(0, 2 * B, B):
            update = jnp.dot(
                operators[f, zone], X[f][:, wave : wave + B], preferred_element_type=F32
            )
            yield
            for part in range(0, 2 * B, B):
                value = X32[f][part : part + B, wave : wave + B] + update[part : part + B]
                Y32[f][wave : wave + B, part : part + B] = value
                Y[f][wave : wave + B, part : part + B] = value.astype(BF16)

    def crossline(level, f):
        zone = zones[level, 1]
        omega = omegas[core * MINE + f]
        for part in range(0, 2 * B, B):
            update = lax.dot_general(
                Y[f][...],
                operators[f, zone, part : part + B, :],
                (((1,), (1,)), ((), ())),
                preferred_element_type=F32,
            )
            yield
            for c in range(0, B, H):
                for r in range(0, B, CH):
                    new = []
                    columns = slice(part + c, part + c + H)
                    for wave in range(0, 2 * B, B):
                        rows = slice(wave + r, wave + r + CH)
                        value = Y32[f][rows, columns] + update[rows, c : c + H]
                        W[f][rows, columns] = value
                        new.append(value)
                    if part > 0:
                        term = W[f][r : r + CH, c : c + H] * W[f][B + r : B + r + CH, c : c + H]
                        term = (term - new[0] * new[1]) * (omega * omega)
                        if f > 0:
                            term += total[c // H, level, r : r + CH, :]
                        total[c // H, level, r : r + CH, :] = term

    def side_by_side(products, others):
        for _ in products:
            for _ in range(PER):
                next(others, None)
        for _ in others:
            pass

    def both(level, f):
        yield from inline(level, f)
        yield from crossline(level, f)

    def one_level(level, carry):
        @pl.when(level < LEVELS)
        def _():
            side_by_side(both(level, 0), rotate(level, 1))

        @pl.when(level >= 0)
        def _():
            following = jnp.minimum(level + 1, LEVELS - 1)
            side_by_side(both(level, 1), rotate(following, 0))

        return carry

    for _ in rotate(0, 0):
        pass
    lax.fori_loop(0, LEVELS, one_level, 0)
    grad_mine[...] = total[core]
    grad_other[...] = total[1 - core].astype(BF16)


def continue_all(omegas, sources, operators, rec_mine, rec_other, mine, other):
    vmem = pl.BlockSpec(memory_space=pltpu.VMEM)
    smem = pl.BlockSpec(memory_space=pltpu.SMEM)
    return pl.pallas_call(
        continue_kernel,
        out_shape=[
            jax.ShapeDtypeStruct((LEVELS, B, H), F32),
            jax.ShapeDtypeStruct((LEVELS, B, H), BF16),
        ],
        in_specs=[smem] + [vmem] * 12,
        out_specs=[vmem, vmem],
        scratch_shapes=[
            pltpu.VMEM((LEVELS, B, B), F32),
            pltpu.SMEM((LEVELS, 2), I32),
            pltpu.VMEM((2, LEVELS, B, H), F32),
            *[pltpu.VMEM((2 * B, 2 * B), kind) for kind in (F32, BF16, F32, BF16, F32) for _ in range(MINE)],
        ],
        compiler_params=pltpu.CompilerParams(vmem_limit_bytes=32 * MB),
        cost_estimate=pl.CostEstimate(
            flops=2 * 128 * B**3, bytes_accessed=8 * MB, transcendentals=0
        ),
        name="continue_levels",
    )(omegas, sources, operators, rec_mine, rec_other, *mine, *other)


def merge_kernel(mine, got, own, s1, s2, s3):
    section, _, _ = place()
    for shift, out in zip(ORDER, (own, s1, s2, s3)):
        level = lax.rem(section + shift, SECTIONS)
        out[...] = (mine[level] + got[level].astype(F32)).astype(out.dtype)


def merge(mine, got):
    vmem = pl.BlockSpec(memory_space=pltpu.VMEM)
    return pl.pallas_call(
        merge_kernel,
        out_shape=[jax.ShapeDtypeStruct((B, H), F32)]
        + [jax.ShapeDtypeStruct((B, H), BF16)] * 3,
        in_specs=[vmem, vmem],
        out_specs=[vmem] * 4,
        compiler_params=pltpu.CompilerParams(vmem_limit_bytes=8 * MB),
        name="merge",
    )(mine, got)


def assemble_kernel(own, g1, g2, g3, out):
    section, _, _ = place()
    for shift, block in zip(ORDER, (own, g1, g2, g3)):
        origin = lax.rem(section + SECTIONS - shift, SECTIONS)
        out[0, pl.ds(pl.multiple_of(origin * B, B), B), :] = block[...].astype(F32)


def assemble(own, blocks):
    vmem = pl.BlockSpec(memory_space=pltpu.VMEM)
    return pl.pallas_call(
        assemble_kernel,
        out_shape=jax.ShapeDtypeStruct((1, SECTIONS * B, H), F32),
        in_specs=[vmem] * 4,
        out_specs=vmem,
        compiler_params=pltpu.CompilerParams(vmem_limit_bytes=8 * MB),
        name="assemble",
    )(own, *blocks)


def along_depth(block, shift):
    return lax.ppermute(block, "depth", [(i, (i + shift) % SECTIONS) for i in range(SECTIONS)])


def all_along_depth(blocks):
    return [along_depth(block, shift) for block, shift in zip(blocks, ORDER[1:])]


def other_core(block):
    count = lax.axis_size("xline")
    return lax.ppermute(block, "xline", [(i, i ^ 1) for i in range(count)])


def per_device(
    receiver_data, source_amp, source_x, source_y, omegas, slowness, inverses, zones_x, zones_y
):
    blocks = pack(slowness, zones_x, zones_y)
    moved = all_along_depth(blocks[1:])
    rec_mine, rec_send, sources = starting_fields(
        receiver_data, source_amp, source_x.reshape(1, -1), source_y.reshape(1, -1), blocks[0]
    )
    own_other = other_core(blocks[0])
    inverses, rec_send, *moved = lax.optimization_barrier((inverses, rec_send, *moved))
    rec_other = other_core(rec_send)
    operators = prepare(inverses)
    mine = [blocks[0], *moved]
    other = [own_other] + [other_core(block) for block in moved]
    grad_mine, grad_other = continue_all(
        omegas, sources, operators, rec_mine, rec_other, mine, other
    )
    own, *parts = merge(grad_mine, other_core(grad_other))
    return assemble(own, all_along_depth(parts))


def solution(mesh):
    in_specs = (
        P(None, None, None, "xline"),
        P(),
        P(),
        P(),
        P(),
        P("depth", None, "xline"),
        P(),
        P("depth", None),
        P("depth", None),
    )
    return jax.shard_map(
        per_device,
        mesh=mesh,
        in_specs=in_specs,
        out_specs=P("depth", None, "xline"),
        check_vma=False,
    )
```

```python
import math

import jax
import jax.numpy as jnp
from jax import lax
from jax.experimental import pallas as pl
from jax.experimental.pallas import tpu as pltpu
from jax.sharding import PartitionSpec as P

F32 = jnp.float32
BF16 = jnp.bfloat16
I32 = jnp.int32
I16 = jnp.int16

SECTIONS = 4
LEVELS = 4
FREQS = 4
MINE = 2
B = 256
H = 128
EXTRA = 16

MIDDLE = 1.1
STEPS = 36000.0

SIN = (4.4428679, -7.30744341, 3.59478797, -0.78437374)
COS = (1.4142135, -6.97885099, 5.73946117, -1.88356295, 0.3106981)

MB = 1 << 20


def horner(u, coefs):
    total = coefs[-1]
    for c in coefs[-2::-1]:
        total = total * u + c
    return total


def place():
    line = lax.axis_index("xline")
    return lax.axis_index("depth"), line // 2, lax.rem(line, 2)


def pack_kernel(slow, zones_x, zones_y, q0, q1, q2, q3, raw, packed, in_sems, out_sems):
    section, pair, _ = place()
    order = ((1, q1), (2, q2), (3, q3), (0, q0))
    arrivals = []
    for shift, _ in order:
        start = pl.ds(pl.multiple_of(lax.rem(section + shift, SECTIONS) * B, B), B)
        arrivals.append(
            pltpu.make_async_copy(slow.at[0, start, :], raw.at[shift], in_sems.at[shift])
        )
        arrivals[-1].start()
    zone_y = zones_y[0, pair]
    upper = lax.broadcasted_iota(I32, (EXTRA, H), 0) < EXTRA // 2
    departures = []
    for (shift, q), arrival in zip(order, arrivals):
        to = lax.rem(section + shift, SECTIONS)
        packed[shift, B:, :] = jnp.where(upper, zones_x[0, to], zone_y).astype(I16)
        arrival.wait()
        for r in range(0, B, 32):
            level = (raw[shift, r : r + 32, :] - MIDDLE) * STEPS
            level = jnp.clip(level, -32767.0, 32767.0)
            packed[shift, r : r + 32, :] = jnp.round(level).astype(I32).astype(I16)
        departures.append(pltpu.make_async_copy(packed.at[shift], q, out_sems.at[shift]))
        departures[-1].start()
    for copy in departures:
        copy.wait()


def pack(slowness, zones_x, zones_y):
    smem = pl.BlockSpec(memory_space=pltpu.SMEM)
    hbm = pl.BlockSpec(memory_space=pl.ANY)
    return pl.pallas_call(
        pack_kernel,
        out_shape=[jax.ShapeDtypeStruct((B + EXTRA, H), I16)] * 4,
        in_specs=[hbm, smem, smem],
        out_specs=[hbm] * 4,
        scratch_shapes=[
            pltpu.VMEM((SECTIONS, B, H), F32),
            pltpu.VMEM((SECTIONS, B + EXTRA, H), I16),
            pltpu.SemaphoreType.DMA((SECTIONS,)),
            pltpu.SemaphoreType.DMA((SECTIONS,)),
        ],
        name="pack",
    )(slowness, zones_x, zones_y)


def fields_kernel(
    receiver, amp_hbm, source_x_hbm, source_y_hbm, _, rec_mine, rec_send, sources,
    rec, amp, source_x, source_y, spread, fields, in_sems, out_sems,
):
    section, pair, core = place()
    rows = pl.ds(pl.multiple_of(section * B, B), B)
    parts = [
        receiver.at[pl.ds(lax.rem(core + 1 - k, 2) * MINE, MINE), :, rows, :] for k in range(2)
    ]
    arrivals = [
        pltpu.make_async_copy(*ends, in_sems.at[k])
        for k, ends in enumerate(
            (
                (amp_hbm, amp),
                (source_x_hbm, source_x),
                (source_y_hbm, source_y),
                (parts[0], rec.at[0]),
                (parts[1], rec.at[1]),
            )
        )
    ]
    for copy in arrivals:
        copy.start()
    departures = [
        pltpu.make_async_copy(*ends, out_sems.at[k])
        for k, ends in enumerate(((rec.at[0], rec_send), (rec.at[1], rec_mine), (fields, sources)))
    ]
    for copy in arrivals:
        copy.wait()
    for copy in departures[:2]:
        copy.start()
    count = source_x.shape[1]
    cells = lax.broadcasted_iota(I32, (B, count), 0)
    hot_x = jnp.where(cells + section * B == source_x[...], 1.0, 0.0).astype(BF16)
    hot_y = cells + pair * B == source_y[...]
    for f in range(MINE):
        for part in range(2):
            row = amp[pl.ds(core * MINE + f, 1), part, :].astype(F32)
            spread[part * B : (part + 1) * B, :] = jnp.where(hot_y, row, 0.0).astype(BF16)
        fields[f] = lax.dot_general(
            hot_x, spread[...], (((1,), (1,)), ((), ())), preferred_element_type=F32
        ).astype(BF16)
    departures[2].start()
    for copy in departures:
        copy.wait()


def starting_fields(receiver, amp, source_x, source_y, after):
    part = jax.ShapeDtypeStruct((MINE, 2, B, H), BF16)
    field = jax.ShapeDtypeStruct((MINE, B, 2 * B), BF16)
    hbm = pl.BlockSpec(memory_space=pl.ANY)
    return pl.pallas_call(
        fields_kernel,
        out_shape=[part, part, field],
        in_specs=[hbm] * 5,
        out_specs=[hbm] * 3,
        scratch_shapes=[
            pltpu.VMEM((2, MINE, 2, B, H), BF16),
            pltpu.VMEM(amp.shape, BF16),
            pltpu.VMEM(source_x.shape, I32),
            pltpu.VMEM(source_y.shape, I32),
            pltpu.VMEM((2 * B, source_x.shape[1]), BF16),
            pltpu.VMEM((MINE, B, 2 * B), BF16),
            pltpu.SemaphoreType.DMA((5,)),
            pltpu.SemaphoreType.DMA((3,)),
        ],
        cost_estimate=pl.CostEstimate(flops=8 * B**3, bytes_accessed=3 * MB, transcendentals=0),
        name="starting_fields",
    )(receiver, amp, source_x, source_y, after)


def prepare_kernel(inverses, operators, table, sems):
    core = place()[2]
    zones = table.shape[1]
    copies = [
        [
            pltpu.make_async_copy(
                inverses.at[core * MINE + f, zone], table.at[f, zone], sems.at[f, zone]
            )
            for zone in range(zones)
        ]
        for f in range(MINE)
    ]
    for f in range(MINE):
        for copy in copies[f]:
            copy.start()
    for f in range(MINE):
        for zone in range(zones):
            copies[f][zone].wait()
            real = table[f, zone, 0]
            imag = table[f, zone, 1]
            operators[f, zone, :B, :B] = real
            operators[f, zone, B:, B:] = real
            operators[f, zone, B:, :B] = imag
            operators[f, zone, :B, B:] = -imag


def prepare(inverses):
    zones = inverses.shape[1]
    return pl.pallas_call(
        prepare_kernel,
        out_shape=jax.ShapeDtypeStruct((MINE, zones, 2 * B, 2 * B), BF16),
        in_specs=[pl.BlockSpec(memory_space=pltpu.HBM)],
        out_specs=pl.BlockSpec(memory_space=pltpu.VMEM),
        scratch_shapes=[
            pltpu.VMEM((MINE, zones, 2, B, B), BF16),
            pltpu.SemaphoreType.DMA((MINE, zones)),
        ],
        compiler_params=pltpu.CompilerParams(vmem_limit_bytes=48 * MB),
        cost_estimate=pl.CostEstimate(flops=0, bytes_accessed=6 * MB, transcendentals=0),
        name="prepare",
    )(inverses)


def continue_kernel(
    omegas, sources, operators, rec_mine, rec_other,
    q0, q1, q2, q3, p0, p1, p2, p3,
    grad_mine, grad_other,
    slow, zones, total, *waves,
):
    section, _, core = place()
    W, X, X32, Y, Y32 = (waves[k : k + MINE] for k in range(0, 5 * MINE, MINE))
    mine = pl.ds(pl.multiple_of(core * H, H), H)
    other = pl.ds(pl.multiple_of((1 - core) * H, H), H)

    for shift, (q, p) in enumerate(((q0, p0), (q1, p1), (q2, p2), (q3, p3))):
        level = lax.rem(section + SECTIONS - shift, SECTIONS)
        for r in range(0, B, 32):
            slow[level, r : r + 32, mine] = q[r : r + 32, :].astype(I32).astype(F32)
            slow[level, r : r + 32, other] = p[r : r + 32, :].astype(I32).astype(F32)
        marks = q[B:, :].astype(I32)
        zones[level, 0] = jnp.max(marks[: EXTRA // 2])
        zones[level, 1] = jnp.max(marks[EXTRA // 2 :])

    for f in range(MINE):
        W[f][:B, :] = sources[f].astype(F32)
        for columns, rec in ((mine, rec_mine), (other, rec_other)):
            W[f][B:, columns] = rec[f, 0].astype(F32)
        imag_mine = pl.ds(pl.multiple_of(B + core * H, H), H)
        imag_other = pl.ds(pl.multiple_of(B + (1 - core) * H, H), H)
        for columns, rec in ((imag_mine, rec_mine), (imag_other, rec_other)):
            W[f][B:, columns] = -rec[f, 1].astype(F32)

    CH, PER = 8, 24

    def rotate(level, f):
        omega = omegas[core * MINE + f]
        scale = omega * (0.5 / math.pi / STEPS)
        base = omega * (0.5 / math.pi * MIDDLE) - 0.5
        for r in range(0, B, CH):
            for c in range(0, B, H):
                turn = slow[level, r : r + CH, c : c + H] * scale + base
                square = turn * turn
                half_sin = turn * horner(square, SIN)
                half_cos = horner(square, COS)
                cosine = half_sin * half_sin - 1.0
                sine = -half_sin * half_cos
                for wave in range(0, 2 * B, B):
                    rows = slice(wave + r, wave + r + CH)
                    columns = slice(wave + c, wave + c + H)
                    real = W[f][rows, c : c + H]
                    imag = W[f][rows, B + c : B + c + H]
                    for down, value in (
                        (r, real * cosine - imag * sine),
                        (B + r, real * sine + imag * cosine),
                    ):
                        X32[f][down : down + CH, columns] = value
                        X[f][down : down + CH, columns] = value.astype(BF16)
                yield

    def inline(level, f):
        zone = zones[level, 0]
        for wave in range(0, 2 * B, B):
            update = jnp.dot(
                operators[f, zone], X[f][:, wave : wave + B], preferred_element_type=F32
            )
            yield
            for part in range(0, 2 * B, B):
                value = X32[f][part : part + B, wave : wave + B] + update[part : part + B]
                Y32[f][wave : wave + B, part : part + B] = value
                Y[f][wave : wave + B, part : part + B] = value.astype(BF16)

    def crossline(level, f):
        zone = zones[level, 1]
        omega = omegas[core * MINE + f]
        for part in range(0, 2 * B, B):
            update = lax.dot_general(
                Y[f][...],
                operators[f, zone, part : part + B, :],
                (((1,), (1,)), ((), ())),
                preferred_element_type=F32,
            )
            yield
            for c in range(0, B, H):
                for r in range(0, B, CH):
                    new = []
                    columns = slice(part + c, part + c + H)
                    for wave in range(0, 2 * B, B):
                        rows = slice(wave + r, wave + r + CH)
                        value = Y32[f][rows, columns] + update[rows, c : c + H]
                        W[f][rows, columns] = value
                        new.append(value)
                    if part > 0:
                        term = W[f][r : r + CH, c : c + H] * W[f][B + r : B + r + CH, c : c + H]
                        term = (term - new[0] * new[1]) * (omega * omega)
                        if f > 0:
                            term += total[c // H, level, r : r + CH, :]
                        total[c // H, level, r : r + CH, :] = term

    def side_by_side(products, others):
        for _ in products:
            for _ in range(PER):
                next(others, None)
        for _ in others:
            pass

    def both(level, f):
        yield from inline(level, f)
        yield from crossline(level, f)

    def one_level(level, carry):
        @pl.when(level < LEVELS)
        def _():
            side_by_side(both(level, 0), rotate(level, 1))

        @pl.when(level >= 0)
        def _():
            following = jnp.minimum(level + 1, LEVELS - 1)
            side_by_side(both(level, 1), rotate(following, 0))

        return carry

    for _ in rotate(0, 0):
        pass
    lax.fori_loop(0, LEVELS, one_level, 0)
    grad_mine[...] = total[core]
    grad_other[...] = total[1 - core].astype(BF16)


def continue_all(omegas, sources, operators, rec_mine, rec_other, mine, other):
    vmem = pl.BlockSpec(memory_space=pltpu.VMEM)
    smem = pl.BlockSpec(memory_space=pltpu.SMEM)
    return pl.pallas_call(
        continue_kernel,
        out_shape=[
            jax.ShapeDtypeStruct((LEVELS, B, H), F32),
            jax.ShapeDtypeStruct((LEVELS, B, H), BF16),
        ],
        in_specs=[smem] + [vmem] * 12,
        out_specs=[vmem, vmem],
        scratch_shapes=[
            pltpu.VMEM((LEVELS, B, B), F32),
            pltpu.SMEM((LEVELS, 2), I32),
            pltpu.VMEM((2, LEVELS, B, H), F32),
            *[pltpu.VMEM((2 * B, 2 * B), kind) for kind in (F32, BF16, F32, BF16, F32) for _ in range(MINE)],
        ],
        compiler_params=pltpu.CompilerParams(vmem_limit_bytes=32 * MB),
        cost_estimate=pl.CostEstimate(
            flops=2 * 128 * B**3, bytes_accessed=8 * MB, transcendentals=0
        ),
        name="continue_levels",
    )(omegas, sources, operators, rec_mine, rec_other, *mine, *other)


def merge_kernel(mine, got, own, s1, s2, s3):
    section, _, _ = place()
    for shift, out in enumerate((own, s1, s2, s3)):
        level = lax.rem(section + shift, SECTIONS)
        out[...] = (mine[level] + got[level].astype(F32)).astype(out.dtype)


def merge(mine, got):
    vmem = pl.BlockSpec(memory_space=pltpu.VMEM)
    return pl.pallas_call(
        merge_kernel,
        out_shape=[jax.ShapeDtypeStruct((B, H), F32)]
        + [jax.ShapeDtypeStruct((B, H), BF16)] * 3,
        in_specs=[vmem, vmem],
        out_specs=[vmem] * 4,
        compiler_params=pltpu.CompilerParams(vmem_limit_bytes=8 * MB),
        name="merge",
    )(mine, got)


def assemble_kernel(own, g1, g2, g3, out):
    section, _, _ = place()
    for shift, block in enumerate((own, g1, g2, g3)):
        origin = lax.rem(section + SECTIONS - shift, SECTIONS)
        out[0, pl.ds(pl.multiple_of(origin * B, B), B), :] = block[...].astype(F32)


def assemble(own, blocks):
    vmem = pl.BlockSpec(memory_space=pltpu.VMEM)
    return pl.pallas_call(
        assemble_kernel,
        out_shape=jax.ShapeDtypeStruct((1, SECTIONS * B, H), F32),
        in_specs=[vmem] * 4,
        out_specs=vmem,
        compiler_params=pltpu.CompilerParams(vmem_limit_bytes=8 * MB),
        name="assemble",
    )(own, *blocks)


def along_depth(block, shift):
    return lax.ppermute(block, "depth", [(i, (i + shift) % SECTIONS) for i in range(SECTIONS)])


def other_core(block):
    count = lax.axis_size("xline")
    return lax.ppermute(block, "xline", [(i, i ^ 1) for i in range(count)])


def per_device(
    receiver_data, source_amp, source_x, source_y, omegas, slowness, inverses, zones_x, zones_y
):
    blocks = pack(slowness, zones_x, zones_y)
    moved = [along_depth(blocks[k], k) for k in (1, 2, 3)]
    rec_mine, rec_send, sources = starting_fields(
        receiver_data, source_amp, source_x.reshape(1, -1), source_y.reshape(1, -1), blocks[0]
    )
    own_other = other_core(blocks[0])
    inverses, sources = lax.optimization_barrier((inverses, sources))
    operators, rec_send, *moved = lax.optimization_barrier(
        (prepare(inverses), rec_send, *moved)
    )
    rec_other = other_core(rec_send)
    mine = [blocks[0], *moved]
    other = [own_other] + [other_core(block) for block in moved]
    grad_mine, grad_other = continue_all(
        omegas, sources, operators, rec_mine, rec_other, mine, other
    )
    own, *parts = merge(grad_mine, other_core(grad_other))
    return assemble(own, [along_depth(parts[k - 1], k) for k in (1, 2, 3)])


def solution(mesh):
    in_specs = (
        P(None, None, None, "xline"),
        P(),
        P(),
        P(),
        P(),
        P("depth", None, "xline"),
        P(),
        P("depth", None),
        P("depth", None),
    )
    return jax.shard_map(
        per_device,
        mesh=mesh,
        in_specs=in_specs,
        out_specs=P("depth", None, "xline"),
        check_vma=False,
    )
```
